32 devices in a mesh: dp: 8 (over y, x, core), win: 4 (over z).
Axes of the slice: x: 2, y: 2, z: 4, core: 2. Of those that a mesh axis runs over, the one named last changes fastest.
Arguments:
- features: bfloat16 [8, 2048, 512], P('dp', 'win')
- upstream_grad: bfloat16 [8, 2048, 256], P('dp', 'win'), may hold values from -48 to 48
- window_of: int32 [8, 2048], P('dp', 'win'), may hold values from 0 to 3, as said below
- window_slot: int32 [8, 2048], P('dp', 'win'), may hold values from 0 to 511
- gain: float32 [512], replicated, may hold values from 0.5 to 1.5
- bias: float32 [512], replicated, may hold values from -3 to 3
- w_qkv: bfloat16 [512, 768], replicated
Outputs:
- grad_in: bfloat16 [8, 2048, 512], P('dp', 'win')
- grad_qkv: float32 [512, 768], replicated
- grad_gain: float32 [512], replicated
- grad_bias: float32 [512], replicated
The draws below stay inside these ranges and needn't reach their ends.
Inputs may be any that keep to these rules, and one draw needn't show every extreme that they name: `window_of`: in every scene each window receives exactly 512 points, whose window_slot values are distinct. The points of one tile (a block of 512 consecutive points) go to one window at most 256 times; every tile sends exactly 256 points to one window, and every window receives 256 points from one tile.
All inputs are finite; a program needn't handle non-finite values.
Results may differ from the reference program's by a relative error of at most 0.017.
Values may be sent and summed in bfloat16 or wider, within the bound.
A program may use at most 64 MiB of HBM per device.

```python
import math
import jax
import jax.numpy as jnp
from jax import lax

D = 512
HEADS = 4
HEAD = 64
P_DEV = 512
BATCH = 8
POINTS = 2048
N_WIN = 4


def scene_routes(base_key, scene_num):
    scene_key = jax.random.fold_in(jax.random.fold_in(base_key, 7), scene_num)
    jitter_key, order_key, owner_key, shuffle_key, slot_key = jax.random.split(scene_key, 5)
    capacity = 2 * P_DEV // N_WIN
    remaining = P_DEV - capacity
    other_peers = N_WIN - 1
    base_count = remaining // other_peers
    extra_count = remaining % other_peers
    counts = base_count + (jnp.arange(other_peers) < extra_count).astype(jnp.int32)
    pair_count = other_peers // 2
    jitter = jax.random.randint(jitter_key, (pair_count,), 0, base_count // 2 + 1).astype(jnp.int32)
    shifts = jnp.zeros((other_peers,), jnp.int32)
    shifts = shifts.at[0:2 * pair_count:2].add(jitter)
    shifts = shifts.at[1:2 * pair_count:2].add(-jitter)
    counts = jax.random.permutation(order_key, counts + shifts)
    by_offset = jnp.concatenate([jnp.full((1,), capacity, jnp.int32), counts.astype(jnp.int32)])
    owner_shift = jax.random.permutation(owner_key, N_WIN).astype(jnp.int32)
    sources = jnp.arange(N_WIN, dtype=jnp.int32)
    offsets = (owner_shift[None, :] - sources[:, None]) % N_WIN
    table = by_offset[offsets]

    def one_source(source_key, row_counts):
        targets = jnp.repeat(jnp.arange(N_WIN, dtype=jnp.int32), row_counts, total_repeat_length=P_DEV)
        return jax.random.permutation(source_key, targets)
    target = jax.vmap(one_source)(jax.random.split(shuffle_key, N_WIN), table).reshape(-1)
    member = (target[None, :] == jnp.arange(N_WIN, dtype=jnp.int32)[:, None]).astype(jnp.int32)
    send_rank = jnp.sum(member * (jnp.cumsum(member, axis=1) - 1), axis=0)

    def one_window(window_key):
        return jax.random.permutation(window_key, P_DEV).astype(jnp.int32)
    slot_perms = jax.vmap(one_window)(jax.random.split(slot_key, N_WIN))
    slots = slot_perms[target, send_rank]
    return (target.astype(jnp.int32), slots.astype(jnp.int32))


def draw_window_of(key, part):

    def first(scene_num):
        return scene_routes(key, scene_num)[0]
    return jax.vmap(first)(jnp.arange(BATCH))


def draw_window_slot(key, part):

    def second(scene_num):
        return scene_routes(key, scene_num)[1]
    return jax.vmap(second)(jnp.arange(BATCH))


def draw_features(key, part):
    base_key, scale_key = jax.random.split(jax.random.fold_in(key, 11), 2)
    shape = (BATCH, POINTS, D)
    base = jax.random.normal(base_key, shape, jnp.float32)
    log_top = math.log(10.0)
    row_scale = jnp.exp(jax.random.uniform(scale_key, (BATCH, POINTS, 1), jnp.float32, 0.0, log_top))
    return (base * row_scale).astype(jnp.bfloat16)


def draw_w_qkv(key, part):
    inner = HEADS * HEAD
    weights = jax.random.normal(jax.random.fold_in(key, 13), (D, 3 * inner), jnp.float32) / math.sqrt(D)
    return weights.astype(jnp.bfloat16)


def levels(rng, shape, cuts, low, largest):
    def one(dim, parts):
        steps = jax.random.uniform(jax.random.fold_in(jax.random.fold_in(rng, 6), dim), (parts,), jnp.float32, low / len(cuts), largest / len(cuts))
        return jnp.repeat(jnp.exp(steps), shape[dim] // parts).reshape((-1,) + (1,) * (len(shape) - dim - 1))

    level = one(*cuts[0])
    for cut in cuts[1:]:
        level = level * one(*cut)
    return level


def scatter_about(key, dims, spread, limit, pieces=(), held_as=jnp.bfloat16):
    level = levels(key, dims, pieces, -0.22, 0.18) if pieces else 1.0
    array = jax.random.normal(key, dims, jnp.float32) * spread * level
    return jnp.minimum(jnp.maximum(array, -limit), limit).astype(held_as)


def setup_inputs(seed: int = 0) -> dict:
    streams_of = jax.random.split(jax.random.key(seed), 8)
    return {
        "features": draw_features(jax.random.fold_in(streams_of[7], 71), 0),
        "upstream_grad": scatter_about(streams_of[1], (BATCH, POINTS, HEADS * HEAD), 8.0, 48.0, ((0, 8), (1, 4))),
        "window_of": draw_window_of(jax.random.fold_in(streams_of[7], 71), 0),
        "window_slot": draw_window_slot(jax.random.fold_in(streams_of[7], 71), 0),
        "gain": jnp.clip(1.0 + 0.1 * jax.random.normal(streams_of[4], (D,), jnp.float32), 0.5, 1.5),
        "bias": scatter_about(streams_of[5], (D,), 0.5, 3.0, (), jnp.float32),
        "w_qkv": draw_w_qkv(jax.random.fold_in(streams_of[7], 71), 0),
    }


epsilon = 1e-05

def normalize(window_rows, gain, bias, w_qkv):
    rows_f = window_rows.astype(jnp.float32)
    row_mean = lax.optimization_barrier(jnp.mean(rows_f, axis=1, keepdims=True))
    centered = rows_f - row_mean
    row_var = lax.optimization_barrier(jnp.mean(centered * centered, axis=1, keepdims=True))
    inv_std = lax.rsqrt(row_var + epsilon)
    unit_rows = centered * inv_std
    normed = (unit_rows * gain + bias).astype(jnp.bfloat16)
    qkv = jnp.dot(normed, w_qkv, preferred_element_type=jnp.float32).astype(jnp.bfloat16)
    return (unit_rows, inv_std, normed, qkv)

def attention_grads(qkv, window_upstream):
    inner = HEADS * HEAD
    score_scale = HEAD ** (-0.5)
    d_queries = []
    d_keys = []
    d_values = []
    for head_num in range(HEADS):
        col_start = head_num * HEAD
        queries = qkv[:, col_start:col_start + HEAD]
        key_block = qkv[:, inner + col_start:inner + col_start + HEAD]
        value_block = qkv[:, 2 * inner + col_start:2 * inner + col_start + HEAD]
        outer = window_upstream[:, col_start:col_start + HEAD]
        scores = jnp.dot(queries, key_block.T, preferred_element_type=jnp.float32) * score_scale
        row_max = lax.optimization_barrier(jnp.max(scores, axis=1, keepdims=True))
        exp_scores = jnp.exp(scores - row_max)
        attn_probs = exp_scores / lax.optimization_barrier(jnp.sum(exp_scores, axis=1, keepdims=True))
        probs_bf = attn_probs.astype(jnp.bfloat16)
        grad_probs = jnp.dot(outer, value_block.T, preferred_element_type=jnp.float32)
        row_delta = lax.optimization_barrier(jnp.sum(attn_probs * grad_probs, axis=1, keepdims=True))
        grad_scores = (attn_probs * (grad_probs - row_delta) * score_scale).astype(jnp.bfloat16)
        d_queries.append(jnp.dot(grad_scores, key_block, preferred_element_type=jnp.float32).astype(jnp.bfloat16))
        d_keys.append(jnp.dot(grad_scores.T, queries, preferred_element_type=jnp.float32).astype(jnp.bfloat16))
        d_values.append(jnp.dot(probs_bf.T, outer, preferred_element_type=jnp.float32).astype(jnp.bfloat16))
    return jnp.concatenate(d_queries + d_keys + d_values, axis=1)

def finish(grad_rows, unit_rows, inv_std, normed, gain, w_qkv):
    grad_weight = jnp.dot(normed.T, grad_rows, preferred_element_type=jnp.float32)
    grad_normed = jnp.dot(grad_rows, w_qkv.T, preferred_element_type=jnp.float32)
    grad_gain = lax.optimization_barrier(jnp.sum(grad_normed * unit_rows, axis=0))
    grad_bias = lax.optimization_barrier(jnp.sum(grad_normed, axis=0))
    grad_hat = grad_normed * gain
    first_mean = lax.optimization_barrier(jnp.mean(grad_hat, axis=1, keepdims=True))
    second_mean = lax.optimization_barrier(jnp.mean(grad_hat * unit_rows, axis=1, keepdims=True))
    grad_window = (inv_std * (grad_hat - first_mean - unit_rows * second_mean)).astype(jnp.bfloat16)
    return (grad_window, grad_weight, grad_gain, grad_bias)

def reference(features, upstream_grad, window_of, window_slot, gain, bias, w_qkv):

    def per_window(totals, window_pair):
        window_rows, window_upstream = window_pair
        unit_rows, inv_std, normed, qkv = normalize(window_rows, gain, bias, w_qkv)
        grad_rows = attention_grads(qkv, window_upstream)
        grad_window, grad_weight, grad_gain, grad_bias = finish(grad_rows, unit_rows, inv_std, normed, gain, w_qkv)
        return ((totals[0] + grad_weight, totals[1] + grad_gain, totals[2] + grad_bias), grad_window)

    def per_scene(totals, scene_inputs):
        scene_feats, scene_up, target, slot_in = scene_inputs
        location = (target * P_DEV + slot_in).astype(jnp.int32)
        rows_all = jnp.zeros_like(scene_feats).at[location].set(scene_feats).reshape(N_WIN, P_DEV, D)
        up_all = jnp.zeros_like(scene_up).at[location].set(scene_up).reshape(N_WIN, P_DEV, HEADS * HEAD)
        totals, grad_windows = lax.scan(per_window, totals, (rows_all, up_all))
        return (totals, grad_windows.reshape(POINTS, D)[location])
    start_sums = (jnp.zeros((D, 3 * HEADS * HEAD), jnp.float32), jnp.zeros((D,), jnp.float32), jnp.zeros((D,), jnp.float32))
    totals, grad_in = lax.scan(per_scene, start_sums, (features, upstream_grad, window_of, window_slot))
    window_count = BATCH * N_WIN
    return (grad_in, totals[0] / window_count, totals[1] / window_count, totals[2] / window_count)
```

```python
import jax
import jax.numpy as jnp
from jax import lax
from jax.experimental import pallas as pl
from jax.experimental.pallas import tpu as pltpu
from jax.sharding import PartitionSpec as P

HEADS = 4
HEAD = 64


epsilon = 1e-05


def normalize(window_rows, gain, bias, w_qkv):
    rows_f = window_rows.astype(jnp.float32)
    row_mean = jnp.mean(rows_f, axis=1, keepdims=True)
    centered = rows_f - row_mean
    row_var = jnp.mean(centered * centered, axis=1, keepdims=True)
    inv_std = lax.rsqrt(row_var + epsilon)
    unit_rows = centered * inv_std
    normed = (unit_rows * gain + bias).astype(jnp.bfloat16)
    qkv = jnp.dot(normed, w_qkv, preferred_element_type=jnp.float32).astype(jnp.bfloat16)
    return (unit_rows, inv_std, normed, qkv)


def attention_grads(qkv, window_upstream):
    inner = HEADS * HEAD
    score_scale = HEAD ** (-0.5)
    d_queries = []
    d_keys = []
    d_values = []
    for head_num in range(HEADS):
        col_start = head_num * HEAD
        queries = qkv[:, col_start : col_start + HEAD]
        key_block = qkv[:, inner + col_start : inner + col_start + HEAD]
        value_block = qkv[:, 2 * inner + col_start : 2 * inner + col_start + HEAD]
        outer = window_upstream[:, col_start : col_start + HEAD]
        scores = jnp.dot(queries, key_block.T, preferred_element_type=jnp.float32) * score_scale
        row_max = jnp.max(scores, axis=1, keepdims=True)
        exp_scores = jnp.exp(scores - row_max)
        attn_probs = exp_scores / jnp.sum(exp_scores, axis=1, keepdims=True)
        probs_bf = attn_probs.astype(jnp.bfloat16)
        grad_probs = jnp.dot(outer, value_block.T, preferred_element_type=jnp.float32)
        row_delta = jnp.sum(attn_probs * grad_probs, axis=1, keepdims=True)
        grad_scores = (attn_probs * (grad_probs - row_delta) * score_scale).astype(jnp.bfloat16)
        d_queries.append(
            jnp.dot(grad_scores, key_block, preferred_element_type=jnp.float32).astype(jnp.bfloat16)
        )
        d_keys.append(
            lax.dot_general(
                grad_scores, queries, (((0,), (0,)), ((), ())), preferred_element_type=jnp.float32
            ).astype(jnp.bfloat16)
        )
        d_values.append(
            lax.dot_general(
                probs_bf, outer, (((0,), (0,)), ((), ())), preferred_element_type=jnp.float32
            ).astype(jnp.bfloat16)
        )
    return jnp.concatenate(d_queries + d_keys + d_values, axis=1)


def finish(grad_rows, unit_rows, inv_std, normed, gain, w_qkv):
    grad_weight = lax.dot_general(
        normed, grad_rows, (((0,), (0,)), ((), ())), preferred_element_type=jnp.float32
    )
    grad_normed = lax.dot_general(
        grad_rows, w_qkv, (((1,), (1,)), ((), ())), preferred_element_type=jnp.float32
    )
    grad_gain = jnp.sum(grad_normed * unit_rows, axis=0)
    grad_bias = jnp.sum(grad_normed, axis=0)
    grad_hat = grad_normed * gain
    first_mean = jnp.mean(grad_hat, axis=1, keepdims=True)
    second_mean = jnp.mean(grad_hat * unit_rows, axis=1, keepdims=True)
    grad_window = (inv_std * (grad_hat - first_mean - unit_rows * second_mean)).astype(jnp.bfloat16)
    return (grad_window, grad_weight, grad_gain, grad_bias)


def per_device(features, upstream_grad, window_of, window_slot, gain, bias, w_qkv):
    win_count = lax.axis_size("win")
    point_count = features.shape[1]
    model_width = features.shape[2]
    inner = upstream_grad.shape[2]
    capacity = 2 * point_count // win_count
    tile_rows = features[0]
    tile_upstream = upstream_grad[0]
    target = window_of[0]
    slot_in = window_slot[0]
    point = jnp.arange(point_count, dtype=jnp.int32)
    earlier = (target[None, :] == target[:, None]) & (point[None, :] < point[:, None])
    send_rank = jnp.sum(earlier.astype(jnp.int32), axis=1)
    position = target * capacity + send_rank
    send_rows = (
        jnp.zeros((win_count * capacity, model_width), jnp.bfloat16).at[position].set(tile_rows)
    )
    send_rows = send_rows.reshape(win_count, capacity, model_width)
    send_slots = jnp.full((win_count * capacity,), point_count, jnp.int32).at[position].set(slot_in)
    send_slots = send_slots.reshape(win_count, capacity)
    send_upstream = (
        jnp.zeros((win_count * capacity, inner), jnp.bfloat16).at[position].set(tile_upstream)
    )
    send_upstream = send_upstream.reshape(win_count, capacity, inner)
    got_rows, got_slots, got_upstream = (
        lax.all_to_all(send_rows, "win", split_axis=0, concat_axis=0, tiled=True),
        lax.all_to_all(send_slots, "win", split_axis=0, concat_axis=0, tiled=True),
        lax.all_to_all(send_upstream, "win", split_axis=0, concat_axis=0, tiled=True),
    )
    flat_slots = got_slots.reshape(-1)
    arrival = (
        jnp.zeros((point_count,), jnp.int32)
        .at[flat_slots]
        .set(jnp.arange(win_count * capacity, dtype=jnp.int32), mode="drop")
    )
    window_rows = got_rows.reshape(-1, model_width)[arrival]
    unit_rows, inv_std, normed, qkv = normalize(window_rows, gain, bias, w_qkv)
    window_upstream = got_upstream.reshape(-1, inner)[arrival]
    grad_rows = attention_grads(qkv, window_upstream)
    grad_window, grad_weight, grad_gain, grad_bias = finish(
        grad_rows, unit_rows, inv_std, normed, gain, w_qkv
    )
    live = (flat_slots < point_count)[:, None]
    safe_slots = jnp.minimum(flat_slots, point_count - 1)
    send_back = jnp.where(live, grad_window[safe_slots], jnp.zeros((), jnp.bfloat16))
    send_back = send_back.reshape(win_count, capacity, model_width)
    returned = lax.all_to_all(send_back, "win", split_axis=0, concat_axis=0, tiled=True)
    grad_in = returned.reshape(-1, model_width)[position]
    total_weight, total_gain, total_bias = lax.psum(
        (grad_weight, grad_gain, grad_bias), ("dp", "win")
    )
    window_count = lax.axis_size("dp") * win_count
    return (
        grad_in[None],
        total_weight / window_count,
        total_gain / window_count,
        total_bias / window_count,
    )


BF = jnp.bfloat16
F32 = jnp.float32
PAIR = 2 * HEAD
NT = (((1,), (1,)), ((), ()))
TN = (((0,), (0,)), ((), ()))

POS, QK, VU, DQK, DV, RZ, GZ, SZ = (4 * i for i in range(8))
R0, R1, R2, G0, G1, G2, S0, S1, S2 = range(32, 41)
N_SEM = 41


def fused(
    feat,
    up,
    pos,
    gain,
    bias,
    w,
    grad_in,
    gw_out,
    gs_out,
    unit,
    normed,
    inv,
    pos_all,
    send_qk,
    send_vu,
    got_qk,
    got_vu,
    hot,
    hot_t,
    win_qk,
    probs,
    d_win,
    send_dqk,
    send_dv,
    got_dqk,
    got_dv,
    rows,
    acc,
    stage,
    rb0,
    rb1,
    rb2,
    rbz,
    total,
    small_send,
    small_got,
    small_z,
    ssem,
    rsem,
):
    n = feat.shape[0]
    half = n // 2
    inner = HEADS * HEAD
    scale = HEAD ** (-0.5)
    dp = lax.axis_index("dp")
    me = lax.axis_index("win")
    c = dp % 2
    bx = (dp // 2) % 2
    by = dp // 4
    peer_c = dp + 1 - 2 * c
    peer_x = dp + 2 - 4 * bx
    peer_y = dp + 4 - 8 * by
    peers = [(me + d) % HEADS for d in (2, 1, 3)]

    def remote(source, target, s, r, where):
        return pltpu.make_async_remote_copy(
            src_ref=source,
            dst_ref=target,
            send_sem=ssem.at[s],
            recv_sem=rsem.at[r],
            device_id=where,
            device_id_type=pl.DeviceIdType.MESH,
        )

    places = [(dp, t) for t in peers] + [(p, me) for p in (peer_c, peer_x, peer_y)]
    barrier = pltpu.get_barrier_semaphore()
    for place in places:
        pl.semaphore_signal(barrier, inc=1, device_id=place, device_id_type=pl.DeviceIdType.MESH)
    pl.semaphore_wait(barrier, len(places))

    def block(ref, t, size):
        return ref.at[pl.ds(pl.multiple_of(t * size, size), size)]

    def exchange(source, target, base, size):
        for t in peers:
            remote(block(source, t, size), block(target, me, size), base + t, base + me, (dp, t)).start()

    def arrived(target, base, size):
        for t in peers:
            remote(block(target, t, size), block(target, t, size), base + t, base + t, (dp, t)).wait_recv()

    for t in peers:
        remote(pos, pos_all.at[me], POS + t, POS + me, (dp, t)).start()
    pos_all[me] = pos[...]

    x = feat[...].astype(F32)
    centered = x - jnp.mean(x, axis=1, keepdims=True)
    inv_std = lax.rsqrt(jnp.mean(centered * centered, axis=1, keepdims=True) + epsilon)
    u = centered * inv_std
    unit[...] = u
    inv[...] = inv_std
    normed[...] = (u * gain[...] + bias[...]).astype(BF)
    qk = jnp.dot(normed[...], w[:, : 2 * inner], preferred_element_type=F32).astype(BF)
    for h in range(HEADS):
        send_qk[h * n : (h + 1) * n, :HEAD] = qk[:, h * HEAD : (h + 1) * HEAD]
        send_qk[h * n : (h + 1) * n, HEAD:] = qk[:, inner + h * HEAD : inner + (h + 1) * HEAD]
    exchange(send_qk, got_qk, QK, n)
    v = jnp.dot(normed[...], w[:, 2 * inner :], preferred_element_type=F32).astype(BF)
    for h in range(HEADS):
        send_vu[h * n : (h + 1) * n, :HEAD] = v[:, h * HEAD : (h + 1) * HEAD]
        send_vu[h * n : (h + 1) * n, HEAD:] = up[:, h * HEAD : (h + 1) * HEAD]
    exchange(send_vu, got_vu, VU, n)
    mine = pl.ds(pl.multiple_of(me * n, n), n)
    got_qk[mine, :] = send_qk[mine, :]
    got_vu[mine, :] = send_vu[mine, :]

    for t in peers:
        remote(pos_all.at[t], pos_all.at[t], POS + t, POS + t, (dp, t)).wait_recv()
    for t in range(HEADS):
        row = jnp.broadcast_to(pos_all[t, 0:1, :], (128, n))
        column = row.astype(F32).T.astype(jnp.int32)
        row = jnp.broadcast_to(pos_all[t, 0:1, :], (n, n))
        slots = lax.broadcasted_iota(jnp.int32, (n, n), 0)
        lanes = lax.broadcasted_iota(jnp.int32, (n, 128), 1)

        @pl.loop(0, HEADS)
        def _(k):
            hot[pl.ds(pl.multiple_of(k * n, n), n), t * n : (t + 1) * n] = jnp.where(
                slots + k * n == row, 1.0, 0.0
            ).astype(BF)

        for j in range(HEADS * n // 128):
            hot_t[t * n : (t + 1) * n, j * 128 : (j + 1) * 128] = jnp.where(
                lanes + j * 128 == column, 1.0, 0.0
            ).astype(BF)

    arrived(got_qk, QK, n)

    @pl.loop(0, HEADS)
    def _(k):
        here = pl.ds(pl.multiple_of(k * n, n), n)
        both = jnp.dot(hot[here, :], got_qk[...], preferred_element_type=F32).astype(BF)
        win_qk[here, :] = both
        s = lax.dot_general(both[:, HEAD:], both[:, :HEAD], NT, preferred_element_type=F32) * scale
        e = jnp.exp(s - jnp.max(s, axis=0, keepdims=True))
        probs[here, :] = e * (1.0 / jnp.sum(e, axis=0, keepdims=True))

    arrived(got_vu, VU, n)

    @pl.loop(0, HEADS)
    def _(k):
        here = pl.ds(pl.multiple_of(k * n, n), n)
        both = jnp.dot(hot[here, :], got_vu[...], preferred_element_type=F32).astype(BF)
        values, outer = both[:, :HEAD], both[:, HEAD:]
        p = probs[here, :]
        d_values = jnp.dot(p.astype(BF), outer, preferred_element_type=F32).astype(BF)
        gp = lax.dot_general(values, outer, NT, preferred_element_type=F32)
        delta = jnp.sum(p * gp, axis=0, keepdims=True)
        gs = (p * (gp - delta) * scale).astype(BF)
        queries, keys = win_qk[here, :HEAD], win_qk[here, HEAD:]
        d_win[here, :HEAD] = lax.dot_general(gs, keys, TN, preferred_element_type=F32).astype(BF)
        d_win[here, HEAD:PAIR] = jnp.dot(gs, queries, preferred_element_type=F32).astype(BF)
        d_win[here, PAIR : PAIR + HEAD] = d_values
        d_win[here, PAIR + HEAD :] = jnp.zeros((n, HEAD), BF)

    def to_tile(t, dqk_ref, dv_ref, slot):
        here = pl.ds(pl.multiple_of(t * n, n), n)
        back = jnp.dot(hot_t[here, :], d_win[...], preferred_element_type=F32).astype(BF)
        dqk_ref[pl.ds(pl.multiple_of(slot * n, n), n), :] = back[:, :PAIR]
        place = pl.ds(pl.multiple_of(slot * half, half), half)
        dv_ref[place, :HEAD] = back[:half, PAIR : PAIR + HEAD]
        dv_ref[place, HEAD:] = back[half:, PAIR : PAIR + HEAD]

    for t in peers:
        to_tile(t, send_dqk, send_dv, t)
        remote(block(send_dqk, t, n), block(got_dqk, me, n), DQK + t, DQK + me, (dp, t)).start()
        remote(block(send_dv, t, half), block(got_dv, me, half), DV + t, DV + me, (dp, t)).start()
    to_tile(me, got_dqk, got_dv, me)
    arrived(got_dqk, DQK, n)
    arrived(got_dv, DV, half)
    for h in range(HEADS):
        rows[:, h * HEAD : (h + 1) * HEAD] = got_dqk[h * n : (h + 1) * n, :HEAD]
        rows[:, inner + h * HEAD : inner + (h + 1) * HEAD] = got_dqk[h * n : (h + 1) * n, HEAD:]
        v_at = 2 * inner + h * HEAD
        rows[:half, v_at : v_at + HEAD] = got_dv[h * half : (h + 1) * half, :HEAD]
        rows[half:, v_at : v_at + HEAD] = got_dv[h * half : (h + 1) * half, HEAD:]

    g = lax.dot_general(normed[...], rows[...], TN, preferred_element_type=F32)
    acc[...] = g
    stage[...] = g.astype(BF)
    depth = acc.shape[0]
    d1, d2, d3, d4 = depth // 2, depth // 4, depth // 8, depth // 32
    b1 = (1 - c) * bx + c * by
    b2 = (1 - c) * by + c * bx
    peer_1 = (1 - c) * peer_x + c * peer_y
    peer_2 = (1 - c) * peer_y + c * peer_x
    off0 = c * d1
    off1 = off0 + b1 * d2
    off2 = off1 + b2 * d3
    off3 = off2 + me * d4

    def at(off, size):
        return pl.ds(pl.multiple_of(off, size), size)

    other0 = at((1 - c) * d1, d1)
    other1 = at(off0 + (1 - b1) * d2, d2)
    other2 = at(off1 + (1 - b2) * d3, d3)

    step0 = remote(stage.at[other0], rb0, R0, R0, (peer_c, me))
    step0.start()

    gn = lax.dot_general(rows[...], w[...], NT, preferred_element_type=F32)
    u = unit[...]
    row_id = lax.broadcasted_iota(jnp.int32, (8, gn.shape[1]), 0)
    small = jnp.where(
        row_id == 0,
        jnp.sum(gn * u, axis=0, keepdims=True),
        jnp.where(row_id == 1, jnp.sum(gn, axis=0, keepdims=True), 0.0),
    )
    small_send[0] = small
    small0 = remote(small_send.at[0], small_got.at[0], S0, S0, (peer_c, me))
    small0.start()
    gh = gn * gain[...]
    first = jnp.mean(gh, axis=1, keepdims=True)
    second = jnp.mean(gh * u, axis=1, keepdims=True)
    grad_in[...] = (inv[...] * (gh - first - u * second)).astype(BF)

    step0.wait()
    keep = at(off0, d1)
    acc[keep, :] += rb0[...].astype(F32)
    stage[keep, :] = acc[keep, :].astype(BF)
    step1 = remote(stage.at[other1], rb1, R1, R1, (peer_1, me))
    step1.start()
    small0.wait()
    small_send[1] = small_send[0] + small_got[0]
    small1 = remote(small_send.at[1], small_got.at[1], S1, S1, (peer_x, me))
    small1.start()

    step1.wait()
    keep = at(off1, d2)
    acc[keep, :] += rb1[...].astype(F32)
    stage[keep, :] = acc[keep, :].astype(BF)
    step2 = remote(stage.at[other2], rb2, R2, R2, (peer_2, me))
    step2.start()
    small1.wait()
    small_send[2] = small_send[1] + small_got[1]
    small2 = remote(small_send.at[2], small_got.at[2], S2, S2, (peer_y, me))
    small2.start()

    step2.wait()
    keep = at(off2, d3)
    acc[keep, :] += rb2[...].astype(F32)
    stage[keep, :] = acc[keep, :].astype(BF)
    for t in peers:
        remote(stage.at[at(off2 + t * d4, d4)], rbz.at[me], RZ + t, RZ + me, (dp, t)).start()
    small2.wait()
    small_send[3] = small_send[2] + small_got[2]
    for t in peers:
        remote(small_send.at[3], small_z.at[me], SZ + t, SZ + me, (dp, t)).start()
    small_z[me] = small_send[3]

    mine = at(off3, d4)
    for t in peers:
        remote(rbz.at[t], rbz.at[t], RZ + t, RZ + t, (dp, t)).wait_recv()
    own = acc[mine, :]
    for t in peers:
        own += rbz[t].astype(F32)
    windows = lax.axis_size("dp") * lax.axis_size("win")
    total[mine, :] = (own * (1.0 / windows)).astype(BF)

    for t in peers:
        remote(total.at[mine], total.at[mine], GZ + t, GZ + me, (dp, t)).start()
    for t in peers:
        there = total.at[at(off2 + t * d4, d4)]
        remote(there, there, GZ + t, GZ + t, (dp, t)).wait_recv()
    back2 = remote(total.at[at(off2, d3)], total.at[at(off2, d3)], G2, G2, (peer_2, me))
    back2.start()
    for t in peers:
        remote(small_z.at[t], small_z.at[t], SZ + t, SZ + t, (dp, t)).wait_recv()
    gs_out[...] = (small_z[0] + small_z[1] + small_z[2] + small_z[3]) * (1.0 / windows)

    back2.wait_send()
    remote(total.at[other2], total.at[other2], G2, G2, (peer_2, me)).wait_recv()
    back1 = remote(total.at[at(off1, d2)], total.at[at(off1, d2)], G1, G1, (peer_1, me))
    back1.start()
    back1.wait_send()
    remote(total.at[other1], total.at[other1], G1, G1, (peer_1, me)).wait_recv()
    back0 = remote(total.at[at(off0, d1)], total.at[at(off0, d1)], G0, G0, (peer_c, me))
    back0.start()
    gw_out[at(off0, d1), :] = total[at(off0, d1), :].astype(F32)
    back0.wait_send()
    remote(total.at[other0], total.at[other0], G0, G0, (peer_c, me)).wait_recv()
    gw_out[other0, :] = total[other0, :].astype(F32)

    for t in peers:
        remote(pos, pos, POS + t, POS + t, (dp, t)).wait_send()
        remote(block(send_qk, t, n), block(send_qk, t, n), QK + t, QK + t, (dp, t)).wait_send()
        remote(block(send_vu, t, n), block(send_vu, t, n), VU + t, VU + t, (dp, t)).wait_send()
        remote(block(send_dqk, t, n), block(send_dqk, t, n), DQK + t, DQK + t, (dp, t)).wait_send()
        remote(block(send_dv, t, half), block(send_dv, t, half), DV + t, DV + t, (dp, t)).wait_send()
        piece = stage.at[at(off2 + t * d4, d4)]
        remote(piece, piece, RZ + t, RZ + t, (dp, t)).wait_send()
        remote(total.at[mine], total.at[mine], GZ + t, GZ + t, (dp, t)).wait_send()
        remote(small_send.at[3], small_send.at[3], SZ + t, SZ + t, (dp, t)).wait_send()


def by_heads(features, upstream_grad, window_of, window_slot, gain, bias, w_qkv):
    n, width = features.shape[1:]
    cols = w_qkv.shape[1]
    all_rows = HEADS * n
    pos = jnp.broadcast_to(window_of * n + window_slot, (8, n))
    vmem = pl.BlockSpec(memory_space=pltpu.VMEM)
    grad_in, grad_w, small = pl.pallas_call(
        fused,
        out_shape=(
            jax.ShapeDtypeStruct((n, width), BF),
            jax.ShapeDtypeStruct((width, cols), F32),
            jax.ShapeDtypeStruct((8, width), F32),
        ),
        in_specs=[vmem] * 6,
        out_specs=(vmem, vmem, vmem),
        scratch_shapes=[
            pltpu.VMEM((n, width), F32),
            pltpu.VMEM((n, width), BF),
            pltpu.VMEM((n, 1), F32),
            pltpu.VMEM((HEADS, 8, n), jnp.int32),
            pltpu.VMEM((all_rows, PAIR), BF),
            pltpu.VMEM((all_rows, PAIR), BF),
            pltpu.VMEM((all_rows, PAIR), BF),
            pltpu.VMEM((all_rows, PAIR), BF),
            pltpu.VMEM((all_rows, all_rows), BF),
            pltpu.VMEM((all_rows, all_rows), BF),
            pltpu.VMEM((all_rows, PAIR), BF),
            pltpu.VMEM((all_rows, n), F32),
            pltpu.VMEM((all_rows, 2 * PAIR), BF),
            pltpu.VMEM((all_rows, PAIR), BF),
            pltpu.VMEM((all_rows // 2, PAIR), BF),
            pltpu.VMEM((all_rows, PAIR), BF),
            pltpu.VMEM((all_rows // 2, PAIR), BF),
            pltpu.VMEM((n, cols), BF),
            pltpu.VMEM((width, cols), F32),
            pltpu.VMEM((width, cols), BF),
            pltpu.VMEM((width // 2, cols), BF),
            pltpu.VMEM((width // 4, cols), BF),
            pltpu.VMEM((width // 8, cols), BF),
            pltpu.VMEM((HEADS, width // 32, cols), BF),
            pltpu.VMEM((width, cols), BF),
            pltpu.VMEM((4, 8, width), F32),
            pltpu.VMEM((3, 8, width), F32),
            pltpu.VMEM((HEADS, 8, width), F32),
            pltpu.SemaphoreType.DMA((N_SEM,)),
            pltpu.SemaphoreType.DMA((N_SEM,)),
        ],
        compiler_params=pltpu.CompilerParams(
            collective_id=0, has_side_effects=True, vmem_limit_bytes=56 * 2**20
        ),
    )(features[0], upstream_grad[0], pos, gain[None], bias[None], w_qkv)
    return grad_in[None], grad_w, small[0], small[1]


def solution(mesh):
    placed = (
        P("dp", "win", None),
        P("dp", "win", None),
        P("dp", "win"),
        P("dp", "win"),
        P(),
        P(),
        P(),
    )
    heads_fit = mesh.shape["win"] == HEADS and mesh.shape["dp"] == 8
    return jax.shard_map(
        by_heads if heads_fit else per_device,
        mesh=mesh,
        in_specs=placed,
        out_specs=(P("dp", "win", None), P(), P(), P()),
        check_vma=False,
    )
```

```python
import jax
import jax.numpy as jnp
from jax import lax
from jax.experimental import pallas as pl
from jax.experimental.pallas import tpu as pltpu
from jax.sharding import PartitionSpec as P

HEADS = 4
HEAD = 64


epsilon = 1e-05


def normalize(window_rows, gain, bias, w_qkv):
    rows_f = window_rows.astype(jnp.float32)
    row_mean = jnp.mean(rows_f, axis=1, keepdims=True)
    centered = rows_f - row_mean
    row_var = jnp.mean(centered * centered, axis=1, keepdims=True)
    inv_std = lax.rsqrt(row_var + epsilon)
    unit_rows = centered * inv_std
    normed = (unit_rows * gain + bias).astype(jnp.bfloat16)
    qkv = jnp.dot(normed, w_qkv, preferred_element_type=jnp.float32).astype(jnp.bfloat16)
    return (unit_rows, inv_std, normed, qkv)


def attention_grads(qkv, window_upstream):
    inner = HEADS * HEAD
    score_scale = HEAD ** (-0.5)
    d_queries = []
    d_keys = []
    d_values = []
    for head_num in range(HEADS):
        col_start = head_num * HEAD
        queries = qkv[:, col_start : col_start + HEAD]
        key_block = qkv[:, inner + col_start : inner + col_start + HEAD]
        value_block = qkv[:, 2 * inner + col_start : 2 * inner + col_start + HEAD]
        outer = window_upstream[:, col_start : col_start + HEAD]
        scores = jnp.dot(queries, key_block.T, preferred_element_type=jnp.float32) * score_scale
        row_max = jnp.max(scores, axis=1, keepdims=True)
        exp_scores = jnp.exp(scores - row_max)
        attn_probs = exp_scores / jnp.sum(exp_scores, axis=1, keepdims=True)
        probs_bf = attn_probs.astype(jnp.bfloat16)
        grad_probs = jnp.dot(outer, value_block.T, preferred_element_type=jnp.float32)
        row_delta = jnp.sum(attn_probs * grad_probs, axis=1, keepdims=True)
        grad_scores = (attn_probs * (grad_probs - row_delta) * score_scale).astype(jnp.bfloat16)
        d_queries.append(
            jnp.dot(grad_scores, key_block, preferred_element_type=jnp.float32).astype(jnp.bfloat16)
        )
        d_keys.append(
            lax.dot_general(
                grad_scores, queries, (((0,), (0,)), ((), ())), preferred_element_type=jnp.float32
            ).astype(jnp.bfloat16)
        )
        d_values.append(
            lax.dot_general(
                probs_bf, outer, (((0,), (0,)), ((), ())), preferred_element_type=jnp.float32
            ).astype(jnp.bfloat16)
        )
    return jnp.concatenate(d_queries + d_keys + d_values, axis=1)


def finish(grad_rows, unit_rows, inv_std, normed, gain, w_qkv):
    grad_weight = lax.dot_general(
        normed, grad_rows, (((0,), (0,)), ((), ())), preferred_element_type=jnp.float32
    )
    grad_normed = lax.dot_general(
        grad_rows, w_qkv, (((1,), (1,)), ((), ())), preferred_element_type=jnp.float32
    )
    grad_gain = jnp.sum(grad_normed * unit_rows, axis=0)
    grad_bias = jnp.sum(grad_normed, axis=0)
    grad_hat = grad_normed * gain
    first_mean = jnp.mean(grad_hat, axis=1, keepdims=True)
    second_mean = jnp.mean(grad_hat * unit_rows, axis=1, keepdims=True)
    grad_window = (inv_std * (grad_hat - first_mean - unit_rows * second_mean)).astype(jnp.bfloat16)
    return (grad_window, grad_weight, grad_gain, grad_bias)


def per_device(features, upstream_grad, window_of, window_slot, gain, bias, w_qkv):
    win_count = lax.axis_size("win")
    point_count = features.shape[1]
    model_width = features.shape[2]
    inner = upstream_grad.shape[2]
    capacity = 2 * point_count // win_count
    tile_rows = features[0]
    tile_upstream = upstream_grad[0]
    target = window_of[0]
    slot_in = window_slot[0]
    point = jnp.arange(point_count, dtype=jnp.int32)
    earlier = (target[None, :] == target[:, None]) & (point[None, :] < point[:, None])
    send_rank = jnp.sum(earlier.astype(jnp.int32), axis=1)
    position = target * capacity + send_rank
    send_rows = (
        jnp.zeros((win_count * capacity, model_width), jnp.bfloat16).at[position].set(tile_rows)
    )
    send_rows = send_rows.reshape(win_count, capacity, model_width)
    send_slots = jnp.full((win_count * capacity,), point_count, jnp.int32).at[position].set(slot_in)
    send_slots = send_slots.reshape(win_count, capacity)
    send_upstream = (
        jnp.zeros((win_count * capacity, inner), jnp.bfloat16).at[position].set(tile_upstream)
    )
    send_upstream = send_upstream.reshape(win_count, capacity, inner)
    got_rows, got_slots, got_upstream = (
        lax.all_to_all(send_rows, "win", split_axis=0, concat_axis=0, tiled=True),
        lax.all_to_all(send_slots, "win", split_axis=0, concat_axis=0, tiled=True),
        lax.all_to_all(send_upstream, "win", split_axis=0, concat_axis=0, tiled=True),
    )
    flat_slots = got_slots.reshape(-1)
    arrival = (
        jnp.zeros((point_count,), jnp.int32)
        .at[flat_slots]
        .set(jnp.arange(win_count * capacity, dtype=jnp.int32), mode="drop")
    )
    window_rows = got_rows.reshape(-1, model_width)[arrival]
    unit_rows, inv_std, normed, qkv = normalize(window_rows, gain, bias, w_qkv)
    window_upstream = got_upstream.reshape(-1, inner)[arrival]
    grad_rows = attention_grads(qkv, window_upstream)
    grad_window, grad_weight, grad_gain, grad_bias = finish(
        grad_rows, unit_rows, inv_std, normed, gain, w_qkv
    )
    live = (flat_slots < point_count)[:, None]
    safe_slots = jnp.minimum(flat_slots, point_count - 1)
    send_back = jnp.where(live, grad_window[safe_slots], jnp.zeros((), jnp.bfloat16))
    send_back = send_back.reshape(win_count, capacity, model_width)
    returned = lax.all_to_all(send_back, "win", split_axis=0, concat_axis=0, tiled=True)
    grad_in = returned.reshape(-1, model_width)[position]
    total_weight, total_gain, total_bias = lax.psum(
        (grad_weight, grad_gain, grad_bias), ("dp", "win")
    )
    window_count = lax.axis_size("dp") * win_count
    return (
        grad_in[None],
        total_weight / window_count,
        total_gain / window_count,
        total_bias / window_count,
    )


BF = jnp.bfloat16
F32 = jnp.float32
PAIR = 2 * HEAD
NT = (((1,), (1,)), ((), ()))
TN = (((0,), (0,)), ((), ()))

POS, QK, U, V, DQK, DV, RZ, GZ, SZ = (4 * i for i in range(9))
R0, R1, R2, G0, G1, G2, S0, S1, S2 = range(36, 45)
N_SEM = 45


def fused(
    feat,
    up,
    pos,
    gain,
    bias,
    w,
    grad_in,
    gw_out,
    gs_out,
    unit,
    normed,
    inv,
    pos_all,
    send_qk,
    send_u,
    send_v,
    got_qk,
    got_u,
    got_v,
    tile_qku,
    tile_v,
    hot,
    hot_t,
    win_qku,
    probs,
    d_val,
    d_win,
    send_dqk,
    send_dv,
    got_dqk,
    got_dv,
    rows,
    acc,
    stage,
    rb0,
    rb1,
    rb2,
    rbz,
    total,
    small_send,
    small_got,
    small_z,
    ssem,
    rsem,
):
    n = feat.shape[0]
    half = n // 2
    inner = HEADS * HEAD
    scale = HEAD ** (-0.5)
    dp = lax.axis_index("dp")
    me = lax.axis_index("win")
    c = dp % 2
    bx = (dp // 2) % 2
    by = dp // 4
    peer_c = dp + 1 - 2 * c
    peer_x = dp + 2 - 4 * bx
    peer_y = dp + 4 - 8 * by
    peers = [(me + d) % HEADS for d in (2, 1, 3)]

    def remote(source, target, s, r, where):
        return pltpu.make_async_remote_copy(
            src_ref=source,
            dst_ref=target,
            send_sem=ssem.at[s],
            recv_sem=rsem.at[r],
            device_id=where,
            device_id_type=pl.DeviceIdType.MESH,
        )

    places = [(dp, t) for t in peers] + [(p, me) for p in (peer_c, peer_x, peer_y)]
    barrier = pltpu.get_barrier_semaphore()
    for place in places:
        pl.semaphore_signal(barrier, inc=1, device_id=place, device_id_type=pl.DeviceIdType.MESH)
    pl.semaphore_wait(barrier, len(places))

    def block(ref, t, size):
        return ref.at[pl.ds(pl.multiple_of(t * size, size), size)]

    def exchange(source, target, base, size):
        for t in peers:
            remote(block(source, t, size), block(target, me, size), base + t, base + me, (dp, t)).start()

    def arrived(target, base, size):
        for t in peers:
            remote(block(target, t, size), block(target, t, size), base + t, base + t, (dp, t)).wait_recv()

    for t in peers:
        remote(pos, pos_all.at[me], POS + t, POS + me, (dp, t)).start()
    pos_all[me] = pos[...]

    for h in range(HEADS):
        send_u[h * half : (h + 1) * half, :HEAD] = up[:half, h * HEAD : (h + 1) * HEAD]
        send_u[h * half : (h + 1) * half, HEAD:] = up[half:, h * HEAD : (h + 1) * HEAD]
    exchange(send_u, got_u, U, half)

    x = feat[...].astype(F32)
    centered = x - jnp.mean(x, axis=1, keepdims=True)
    inv_std = lax.rsqrt(jnp.mean(centered * centered, axis=1, keepdims=True) + epsilon)
    u = centered * inv_std
    unit[...] = u
    inv[...] = inv_std
    normed[...] = (u * gain[...] + bias[...]).astype(BF)
    qk = jnp.dot(normed[...], w[:, : 2 * inner], preferred_element_type=F32).astype(BF)
    for h in range(HEADS):
        send_qk[h * n : (h + 1) * n, :HEAD] = qk[:, h * HEAD : (h + 1) * HEAD]
        send_qk[h * n : (h + 1) * n, HEAD:] = qk[:, inner + h * HEAD : inner + (h + 1) * HEAD]
    exchange(send_qk, got_qk, QK, n)
    v = jnp.dot(normed[...], w[:, 2 * inner :], preferred_element_type=F32).astype(BF)
    for h in range(HEADS):
        send_v[h * half : (h + 1) * half, :HEAD] = v[:half, h * HEAD : (h + 1) * HEAD]
        send_v[h * half : (h + 1) * half, HEAD:] = v[half:, h * HEAD : (h + 1) * HEAD]
    exchange(send_v, got_v, V, half)
    mine = pl.ds(pl.multiple_of(me * n, n), n)
    got_qk[mine, :] = send_qk[mine, :]
    mine = pl.ds(pl.multiple_of(me * half, half), half)
    got_u[mine, :] = send_u[mine, :]
    got_v[mine, :] = send_v[mine, :]

    for t in peers:
        remote(pos_all.at[t], pos_all.at[t], POS + t, POS + t, (dp, t)).wait_recv()
    for t in range(HEADS):
        row = jnp.broadcast_to(pos_all[t, 0:1, :], (128, n))
        column = row.astype(F32).T.astype(jnp.int32)
        row = jnp.broadcast_to(pos_all[t, 0:1, :], (n, n))
        slots = lax.broadcasted_iota(jnp.int32, (n, n), 0)
        lanes = lax.broadcasted_iota(jnp.int32, (n, 128), 1)

        @pl.loop(0, HEADS)
        def _(k):
            hot[pl.ds(pl.multiple_of(k * n, n), n), t * n : (t + 1) * n] = jnp.where(
                slots + k * n == row, 1.0, 0.0
            ).astype(BF)

        for j in range(HEADS * n // 128):
            hot_t[t * n : (t + 1) * n, j * 128 : (j + 1) * 128] = jnp.where(
                lanes + j * 128 == column, 1.0, 0.0
            ).astype(BF)

    arrived(got_u, U, half)
    for t in range(HEADS):
        packed = got_u[t * half : (t + 1) * half, :]
        tile_qku[t * n : t * n + half, PAIR : PAIR + HEAD] = packed[:, :HEAD]
        tile_qku[t * n + half : (t + 1) * n, PAIR : PAIR + HEAD] = packed[:, HEAD:]
    tile_qku[:, PAIR + HEAD :] = jnp.zeros((HEADS * n, HEAD), BF)
    arrived(got_qk, QK, n)
    tile_qku[:, :PAIR] = got_qk[...]

    @pl.loop(0, HEADS)
    def _(k):
        here = pl.ds(pl.multiple_of(k * n, n), n)
        three = jnp.dot(hot[here, :], tile_qku[...], preferred_element_type=F32).astype(BF)
        win_qku[here, :] = three
        queries, keys = three[:, :HEAD], three[:, HEAD:PAIR]
        s = lax.dot_general(keys, queries, NT, preferred_element_type=F32) * scale
        e = jnp.exp(s - jnp.max(s, axis=0, keepdims=True))
        p = e * (1.0 / jnp.sum(e, axis=0, keepdims=True))
        probs[here, :] = p
        d_val[here, :] = jnp.dot(
            p.astype(BF), three[:, PAIR : PAIR + HEAD], preferred_element_type=F32
        ).astype(BF)

    def value_rows(t, target):
        here = pl.ds(pl.multiple_of(t * n, n), n)
        back = jnp.dot(hot_t[here, :], d_val[...], preferred_element_type=F32).astype(BF)
        place = pl.ds(pl.multiple_of(t * half, half), half)
        target[place, :HEAD] = back[:half]
        target[place, HEAD:] = back[half:]

    for t in peers:
        value_rows(t, send_dv)
        remote(block(send_dv, t, half), block(got_dv, me, half), DV + t, DV + me, (dp, t)).start()
    value_rows(me, got_dv)

    arrived(got_v, V, half)
    for t in range(HEADS):
        packed = got_v[t * half : (t + 1) * half, :]
        tile_v[t * n : t * n + half, :] = packed[:, :HEAD]
        tile_v[t * n + half : (t + 1) * n, :] = packed[:, HEAD:]

    @pl.loop(0, HEADS)
    def _(k):
        here = pl.ds(pl.multiple_of(k * n, n), n)
        values = jnp.dot(hot[here, :], tile_v[...], preferred_element_type=F32).astype(BF)
        three = win_qku[here, :]
        p = probs[here, :]
        gp = lax.dot_general(
            values, three[:, PAIR : PAIR + HEAD], NT, preferred_element_type=F32
        )
        delta = jnp.sum(p * gp, axis=0, keepdims=True)
        gs = (p * (gp - delta) * scale).astype(BF)
        queries, keys = three[:, :HEAD], three[:, HEAD:PAIR]
        d_win[here, :HEAD] = lax.dot_general(gs, keys, TN, preferred_element_type=F32).astype(BF)
        d_win[here, HEAD:] = jnp.dot(gs, queries, preferred_element_type=F32).astype(BF)

    def to_tile(t, target):
        here = pl.ds(pl.multiple_of(t * n, n), n)
        target[here, :] = jnp.dot(
            hot_t[here, :], d_win[...], preferred_element_type=F32
        ).astype(BF)

    for t in peers:
        to_tile(t, send_dqk)
        remote(block(send_dqk, t, n), block(got_dqk, me, n), DQK + t, DQK + me, (dp, t)).start()
    to_tile(me, got_dqk)
    arrived(got_dv, DV, half)
    arrived(got_dqk, DQK, n)
    for h in range(HEADS):
        rows[:, h * HEAD : (h + 1) * HEAD] = got_dqk[h * n : (h + 1) * n, :HEAD]
        rows[:, inner + h * HEAD : inner + (h + 1) * HEAD] = got_dqk[h * n : (h + 1) * n, HEAD:]
        v_at = 2 * inner + h * HEAD
        rows[:half, v_at : v_at + HEAD] = got_dv[h * half : (h + 1) * half, :HEAD]
        rows[half:, v_at : v_at + HEAD] = got_dv[h * half : (h + 1) * half, HEAD:]

    g = lax.dot_general(normed[...], rows[...], TN, preferred_element_type=F32)
    acc[...] = g
    stage[...] = g.astype(BF)
    depth = acc.shape[0]
    d1, d2, d3, d4 = depth // 2, depth // 4, depth // 8, depth // 32
    b1 = (1 - c) * bx + c * by
    b2 = (1 - c) * by + c * bx
    peer_1 = (1 - c) * peer_x + c * peer_y
    peer_2 = (1 - c) * peer_y + c * peer_x
    off0 = c * d1
    off1 = off0 + b1 * d2
    off2 = off1 + b2 * d3
    off3 = off2 + me * d4

    def at(off, size):
        return pl.ds(pl.multiple_of(off, size), size)

    other0 = at((1 - c) * d1, d1)
    other1 = at(off0 + (1 - b1) * d2, d2)
    other2 = at(off1 + (1 - b2) * d3, d3)

    step0 = remote(stage.at[other0], rb0, R0, R0, (peer_c, me))
    step0.start()

    gn = lax.dot_general(rows[...], w[...], NT, preferred_element_type=F32)
    u = unit[...]
    row_id = lax.broadcasted_iota(jnp.int32, (8, gn.shape[1]), 0)
    small = jnp.where(
        row_id == 0,
        jnp.sum(gn * u, axis=0, keepdims=True),
        jnp.where(row_id == 1, jnp.sum(gn, axis=0, keepdims=True), 0.0),
    )
    small_send[0] = small
    small0 = remote(small_send.at[0], small_got.at[0], S0, S0, (peer_c, me))
    small0.start()
    gh = gn * gain[...]
    first = jnp.mean(gh, axis=1, keepdims=True)
    second = jnp.mean(gh * u, axis=1, keepdims=True)
    grad_in[...] = (inv[...] * (gh - first - u * second)).astype(BF)

    step0.wait()
    keep = at(off0, d1)
    acc[keep, :] += rb0[...].astype(F32)
    stage[keep, :] = acc[keep, :].astype(BF)
    step1 = remote(stage.at[other1], rb1, R1, R1, (peer_1, me))
    step1.start()
    small0.wait()
    small_send[1] = small_send[0] + small_got[0]
    small1 = remote(small_send.at[1], small_got.at[1], S1, S1, (peer_x, me))
    small1.start()

    step1.wait()
    keep = at(off1, d2)
    acc[keep, :] += rb1[...].astype(F32)
    stage[keep, :] = acc[keep, :].astype(BF)
    step2 = remote(stage.at[other2], rb2, R2, R2, (peer_2, me))
    step2.start()
    small1.wait()
    small_send[2] = small_send[1] + small_got[1]
    small2 = remote(small_send.at[2], small_got.at[2], S2, S2, (peer_y, me))
    small2.start()

    step2.wait()
    keep = at(off2, d3)
    acc[keep, :] += rb2[...].astype(F32)
    stage[keep, :] = acc[keep, :].astype(BF)
    for t in peers:
        remote(stage.at[at(off2 + t * d4, d4)], rbz.at[me], RZ + t, RZ + me, (dp, t)).start()
    small2.wait()
    small_send[3] = small_send[2] + small_got[2]
    for t in peers:
        remote(small_send.at[3], small_z.at[me], SZ + t, SZ + me, (dp, t)).start()
    small_z[me] = small_send[3]

    mine = at(off3, d4)
    for t in peers:
        remote(rbz.at[t], rbz.at[t], RZ + t, RZ + t, (dp, t)).wait_recv()
    own = acc[mine, :]
    for t in peers:
        own += rbz[t].astype(F32)
    windows = lax.axis_size("dp") * lax.axis_size("win")
    total[mine, :] = (own * (1.0 / windows)).astype(BF)

    for t in peers:
        remote(total.at[mine], total.at[mine], GZ + t, GZ + me, (dp, t)).start()
    for t in peers:
        there = total.at[at(off2 + t * d4, d4)]
        remote(there, there, GZ + t, GZ + t, (dp, t)).wait_recv()
    back2 = remote(total.at[at(off2, d3)], total.at[at(off2, d3)], G2, G2, (peer_2, me))
    back2.start()
    for t in peers:
        remote(small_z.at[t], small_z.at[t], SZ + t, SZ + t, (dp, t)).wait_recv()
    gs_out[...] = (small_z[0] + small_z[1] + small_z[2] + small_z[3]) * (1.0 / windows)

    back2.wait_send()
    remote(total.at[other2], total.at[other2], G2, G2, (peer_2, me)).wait_recv()
    back1 = remote(total.at[at(off1, d2)], total.at[at(off1, d2)], G1, G1, (peer_1, me))
    back1.start()
    back1.wait_send()
    remote(total.at[other1], total.at[other1], G1, G1, (peer_1, me)).wait_recv()
    back0 = remote(total.at[at(off0, d1)], total.at[at(off0, d1)], G0, G0, (peer_c, me))
    back0.start()
    gw_out[at(off0, d1), :] = total[at(off0, d1), :]
    back0.wait_send()
    remote(total.at[other0], total.at[other0], G0, G0, (peer_c, me)).wait_recv()
    gw_out[other0, :] = total[other0, :]

    for t in peers:
        remote(pos, pos, POS + t, POS + t, (dp, t)).wait_send()
        remote(block(send_qk, t, n), block(send_qk, t, n), QK + t, QK + t, (dp, t)).wait_send()
        remote(block(send_u, t, half), block(send_u, t, half), U + t, U + t, (dp, t)).wait_send()
        remote(block(send_v, t, half), block(send_v, t, half), V + t, V + t, (dp, t)).wait_send()
        remote(block(send_dqk, t, n), block(send_dqk, t, n), DQK + t, DQK + t, (dp, t)).wait_send()
        remote(block(send_dv, t, half), block(send_dv, t, half), DV + t, DV + t, (dp, t)).wait_send()
        piece = stage.at[at(off2 + t * d4, d4)]
        remote(piece, piece, RZ + t, RZ + t, (dp, t)).wait_send()
        remote(total.at[mine], total.at[mine], GZ + t, GZ + t, (dp, t)).wait_send()
        remote(small_send.at[3], small_send.at[3], SZ + t, SZ + t, (dp, t)).wait_send()


def by_heads(features, upstream_grad, window_of, window_slot, gain, bias, w_qkv):
    n, width = features.shape[1:]
    cols = w_qkv.shape[1]
    all_rows = HEADS * n
    pos = jnp.broadcast_to(window_of * n + window_slot, (8, n))
    vmem = pl.BlockSpec(memory_space=pltpu.VMEM)
    grad_in, grad_w, small = pl.pallas_call(
        fused,
        out_shape=(
            jax.ShapeDtypeStruct((n, width), BF),
            jax.ShapeDtypeStruct((width, cols), BF),
            jax.ShapeDtypeStruct((8, width), F32),
        ),
        in_specs=[vmem] * 6,
        out_specs=(vmem, vmem, vmem),
        scratch_shapes=[
            pltpu.VMEM((n, width), F32),
            pltpu.VMEM((n, width), BF),
            pltpu.VMEM((n, 1), F32),
            pltpu.VMEM((HEADS, 8, n), jnp.int32),
            pltpu.VMEM((all_rows, PAIR), BF),
            pltpu.VMEM((all_rows // 2, PAIR), BF),
            pltpu.VMEM((all_rows // 2, PAIR), BF),
            pltpu.VMEM((all_rows, PAIR), BF),
            pltpu.VMEM((all_rows // 2, PAIR), BF),
            pltpu.VMEM((all_rows // 2, PAIR), BF),
            pltpu.VMEM((all_rows, 2 * PAIR), BF),
            pltpu.VMEM((all_rows, HEAD), BF),
            pltpu.VMEM((all_rows, all_rows), BF),
            pltpu.VMEM((all_rows, all_rows), BF),
            pltpu.VMEM((all_rows, 2 * PAIR), BF),
            pltpu.VMEM((all_rows, n), F32),
            pltpu.VMEM((all_rows, HEAD), BF),
            pltpu.VMEM((all_rows, PAIR), BF),
            pltpu.VMEM((all_rows, PAIR), BF),
            pltpu.VMEM((all_rows // 2, PAIR), BF),
            pltpu.VMEM((all_rows, PAIR), BF),
            pltpu.VMEM((all_rows // 2, PAIR), BF),
            pltpu.VMEM((n, cols), BF),
            pltpu.VMEM((width, cols), F32),
            pltpu.VMEM((width, cols), BF),
            pltpu.VMEM((width // 2, cols), BF),
            pltpu.VMEM((width // 4, cols), BF),
            pltpu.VMEM((width // 8, cols), BF),
            pltpu.VMEM((HEADS, width // 32, cols), BF),
            pltpu.VMEM((width, cols), BF),
            pltpu.VMEM((4, 8, width), F32),
            pltpu.VMEM((3, 8, width), F32),
            pltpu.VMEM((HEADS, 8, width), F32),
            pltpu.SemaphoreType.DMA((N_SEM,)),
            pltpu.SemaphoreType.DMA((N_SEM,)),
        ],
        compiler_params=pltpu.CompilerParams(
            collective_id=0, has_side_effects=True, vmem_limit_bytes=56 * 2**20
        ),
    )(features[0], upstream_grad[0], pos, gain[None], bias[None], w_qkv)
    return grad_in[None], grad_w.astype(F32), small[0], small[1]


def solution(mesh):
    placed = (
        P("dp", "win", None),
        P("dp", "win", None),
        P("dp", "win"),
        P("dp", "win"),
        P(),
        P(),
        P(),
    )
    heads_fit = mesh.shape["win"] == HEADS and mesh.shape["dp"] == 8
    return jax.shard_map(
        by_heads if heads_fit else per_device,
        mesh=mesh,
        in_specs=placed,
        out_specs=(P("dp", "win", None), P(), P(), P()),
        check_vma=False,
    )
```

```python
import jax
import jax.numpy as jnp
from jax import lax
from jax.experimental import pallas as pl
from jax.experimental.pallas import tpu as pltpu
from jax.sharding import PartitionSpec as P

HEADS = 4
HEAD = 64


epsilon = 1e-05


def normalize(window_rows, gain, bias, w_qkv):
    rows_f = window_rows.astype(jnp.float32)
    row_mean = jnp.mean(rows_f, axis=1, keepdims=True)
    centered = rows_f - row_mean
    row_var = jnp.mean(centered * centered, axis=1, keepdims=True)
    inv_std = lax.rsqrt(row_var + epsilon)
    unit_rows = centered * inv_std
    normed = (unit_rows * gain + bias).astype(jnp.bfloat16)
    qkv = jnp.dot(normed, w_qkv, preferred_element_type=jnp.float32).astype(jnp.bfloat16)
    return (unit_rows, inv_std, normed, qkv)


def attention_grads(qkv, window_upstream):
    inner = HEADS * HEAD
    score_scale = HEAD ** (-0.5)
    d_queries = []
    d_keys = []
    d_values = []
    for head_num in range(HEADS):
        col_start = head_num * HEAD
        queries = qkv[:, col_start : col_start + HEAD]
        key_block = qkv[:, inner + col_start : inner + col_start + HEAD]
        value_block = qkv[:, 2 * inner + col_start : 2 * inner + col_start + HEAD]
        outer = window_upstream[:, col_start : col_start + HEAD]
        scores = jnp.dot(queries, key_block.T, preferred_element_type=jnp.float32) * score_scale
        row_max = jnp.max(scores, axis=1, keepdims=True)
        exp_scores = jnp.exp(scores - row_max)
        attn_probs = exp_scores / jnp.sum(exp_scores, axis=1, keepdims=True)
        probs_bf = attn_probs.astype(jnp.bfloat16)
        grad_probs = jnp.dot(outer, value_block.T, preferred_element_type=jnp.float32)
        row_delta = jnp.sum(attn_probs * grad_probs, axis=1, keepdims=True)
        grad_scores = (attn_probs * (grad_probs - row_delta) * score_scale).astype(jnp.bfloat16)
        d_queries.append(
            jnp.dot(grad_scores, key_block, preferred_element_type=jnp.float32).astype(jnp.bfloat16)
        )
        d_keys.append(
            lax.dot_general(
                grad_scores, queries, (((0,), (0,)), ((), ())), preferred_element_type=jnp.float32
            ).astype(jnp.bfloat16)
        )
        d_values.append(
            lax.dot_general(
                probs_bf, outer, (((0,), (0,)), ((), ())), preferred_element_type=jnp.float32
            ).astype(jnp.bfloat16)
        )
    return jnp.concatenate(d_queries + d_keys + d_values, axis=1)


def finish(grad_rows, unit_rows, inv_std, normed, gain, w_qkv):
    grad_weight = lax.dot_general(
        normed, grad_rows, (((0,), (0,)), ((), ())), preferred_element_type=jnp.float32
    )
    grad_normed = lax.dot_general(
        grad_rows, w_qkv, (((1,), (1,)), ((), ())), preferred_element_type=jnp.float32
    )
    grad_gain = jnp.sum(grad_normed * unit_rows, axis=0)
    grad_bias = jnp.sum(grad_normed, axis=0)
    grad_hat = grad_normed * gain
    first_mean = jnp.mean(grad_hat, axis=1, keepdims=True)
    second_mean = jnp.mean(grad_hat * unit_rows, axis=1, keepdims=True)
    grad_window = (inv_std * (grad_hat - first_mean - unit_rows * second_mean)).astype(jnp.bfloat16)
    return (grad_window, grad_weight, grad_gain, grad_bias)


def per_device(features, upstream_grad, window_of, window_slot, gain, bias, w_qkv):
    win_count = lax.axis_size("win")
    point_count = features.shape[1]
    model_width = features.shape[2]
    inner = upstream_grad.shape[2]
    capacity = 2 * point_count // win_count
    tile_rows = features[0]
    tile_upstream = upstream_grad[0]
    target = window_of[0]
    slot_in = window_slot[0]
    point = jnp.arange(point_count, dtype=jnp.int32)
    earlier = (target[None, :] == target[:, None]) & (point[None, :] < point[:, None])
    send_rank = jnp.sum(earlier.astype(jnp.int32), axis=1)
    position = target * capacity + send_rank
    send_rows = (
        jnp.zeros((win_count * capacity, model_width), jnp.bfloat16).at[position].set(tile_rows)
    )
    send_rows = send_rows.reshape(win_count, capacity, model_width)
    send_slots = jnp.full((win_count * capacity,), point_count, jnp.int32).at[position].set(slot_in)
    send_slots = send_slots.reshape(win_count, capacity)
    send_upstream = (
        jnp.zeros((win_count * capacity, inner), jnp.bfloat16).at[position].set(tile_upstream)
    )
    send_upstream = send_upstream.reshape(win_count, capacity, inner)
    got_rows, got_slots, got_upstream = (
        lax.all_to_all(send_rows, "win", split_axis=0, concat_axis=0, tiled=True),
        lax.all_to_all(send_slots, "win", split_axis=0, concat_axis=0, tiled=True),
        lax.all_to_all(send_upstream, "win", split_axis=0, concat_axis=0, tiled=True),
    )
    flat_slots = got_slots.reshape(-1)
    arrival = (
        jnp.zeros((point_count,), jnp.int32)
        .at[flat_slots]
        .set(jnp.arange(win_count * capacity, dtype=jnp.int32), mode="drop")
    )
    window_rows = got_rows.reshape(-1, model_width)[arrival]
    unit_rows, inv_std, normed, qkv = normalize(window_rows, gain, bias, w_qkv)
    window_upstream = got_upstream.reshape(-1, inner)[arrival]
    grad_rows = attention_grads(qkv, window_upstream)
    grad_window, grad_weight, grad_gain, grad_bias = finish(
        grad_rows, unit_rows, inv_std, normed, gain, w_qkv
    )
    live = (flat_slots < point_count)[:, None]
    safe_slots = jnp.minimum(flat_slots, point_count - 1)
    send_back = jnp.where(live, grad_window[safe_slots], jnp.zeros((), jnp.bfloat16))
    send_back = send_back.reshape(win_count, capacity, model_width)
    returned = lax.all_to_all(send_back, "win", split_axis=0, concat_axis=0, tiled=True)
    grad_in = returned.reshape(-1, model_width)[position]
    total_weight, total_gain, total_bias = lax.psum(
        (grad_weight, grad_gain, grad_bias), ("dp", "win")
    )
    window_count = lax.axis_size("dp") * win_count
    return (
        grad_in[None],
        total_weight / window_count,
        total_gain / window_count,
        total_bias / window_count,
    )


BF = jnp.bfloat16
F32 = jnp.float32
PAIR = 2 * HEAD
NT = (((1,), (1,)), ((), ()))
TN = (((0,), (0,)), ((), ()))

POS, QK, U, V, DQK, DV, SZ = (4 * i for i in range(7))
S0, S1, S2 = 28, 29, 30
R0, R1, R2, G0, G1, G2 = (31 + 3 * i for i in range(6))
RZ, GZ = 49, 61
N_SEM = 73


def fused(
    feat,
    up,
    pos,
    gain,
    bias,
    w,
    grad_in,
    gw_out,
    gs_out,
    unit,
    normed,
    inv,
    pos_all,
    send_qk,
    send_u,
    send_v,
    got_qk,
    got_u,
    got_v,
    tile_qku,
    tile_v,
    hot,
    hot_t,
    win_qku,
    probs,
    d_val,
    d_win,
    send_dqk,
    send_dv,
    got_dqk,
    got_dv,
    rows,
    acc,
    stage,
    rb0,
    rb1,
    rb2,
    rbz,
    total,
    small_send,
    small_got,
    small_z,
    ssem,
    rsem,
):
    n = feat.shape[0]
    half = n // 2
    inner = HEADS * HEAD
    scale = HEAD ** (-0.5)
    dp = lax.axis_index("dp")
    me = lax.axis_index("win")
    c = dp % 2
    bx = (dp // 2) % 2
    by = dp // 4
    peer_c = dp + 1 - 2 * c
    peer_x = dp + 2 - 4 * bx
    peer_y = dp + 4 - 8 * by
    peers = [(me + d) % HEADS for d in (2, 1, 3)]

    def remote(source, target, s, r, where):
        return pltpu.make_async_remote_copy(
            src_ref=source,
            dst_ref=target,
            send_sem=ssem.at[s],
            recv_sem=rsem.at[r],
            device_id=where,
            device_id_type=pl.DeviceIdType.MESH,
        )

    places = [(dp, t) for t in peers] + [(p, me) for p in (peer_c, peer_x, peer_y)]
    barrier = pltpu.get_barrier_semaphore()
    for place in places:
        pl.semaphore_signal(barrier, inc=1, device_id=place, device_id_type=pl.DeviceIdType.MESH)
    pl.semaphore_wait(barrier, len(places))

    def block(ref, t, size):
        return ref.at[pl.ds(pl.multiple_of(t * size, size), size)]

    def exchange(source, target, base, size):
        for t in peers:
            remote(block(source, t, size), block(target, me, size), base + t, base + me, (dp, t)).start()

    def arrived(target, base, size):
        for t in peers:
            remote(block(target, t, size), block(target, t, size), base + t, base + t, (dp, t)).wait_recv()

    for t in peers:
        remote(pos, pos_all.at[me], POS + t, POS + me, (dp, t)).start()
    pos_all[me] = pos[...]

    for h in range(HEADS):
        send_u[h * half : (h + 1) * half, :HEAD] = up[:half, h * HEAD : (h + 1) * HEAD]
        send_u[h * half : (h + 1) * half, HEAD:] = up[half:, h * HEAD : (h + 1) * HEAD]
    exchange(send_u, got_u, U, half)

    x = feat[...].astype(F32)
    centered = x - jnp.mean(x, axis=1, keepdims=True)
    inv_std = lax.rsqrt(jnp.mean(centered * centered, axis=1, keepdims=True) + epsilon)
    u = centered * inv_std
    unit[...] = u
    inv[...] = inv_std
    normed[...] = (u * gain[...] + bias[...]).astype(BF)
    qk = jnp.dot(normed[...], w[:, : 2 * inner], preferred_element_type=F32).astype(BF)
    for h in range(HEADS):
        send_qk[h * n : (h + 1) * n, :HEAD] = qk[:, h * HEAD : (h + 1) * HEAD]
        send_qk[h * n : (h + 1) * n, HEAD:] = qk[:, inner + h * HEAD : inner + (h + 1) * HEAD]
    exchange(send_qk, got_qk, QK, n)
    v = jnp.dot(normed[...], w[:, 2 * inner :], preferred_element_type=F32).astype(BF)
    for h in range(HEADS):
        send_v[h * half : (h + 1) * half, :HEAD] = v[:half, h * HEAD : (h + 1) * HEAD]
        send_v[h * half : (h + 1) * half, HEAD:] = v[half:, h * HEAD : (h + 1) * HEAD]
    exchange(send_v, got_v, V, half)
    mine = pl.ds(pl.multiple_of(me * n, n), n)
    got_qk[mine, :] = send_qk[mine, :]
    mine = pl.ds(pl.multiple_of(me * half, half), half)
    got_u[mine, :] = send_u[mine, :]
    got_v[mine, :] = send_v[mine, :]

    for t in peers:
        remote(pos_all.at[t], pos_all.at[t], POS + t, POS + t, (dp, t)).wait_recv()
    for t in range(HEADS):
        row = jnp.broadcast_to(pos_all[t, 0:1, :], (128, n))
        column = row.astype(F32).T.astype(jnp.int32)
        row = jnp.broadcast_to(pos_all[t, 0:1, :], (n, n))
        slots = lax.broadcasted_iota(jnp.int32, (n, n), 0)
        lanes = lax.broadcasted_iota(jnp.int32, (n, 128), 1)

        @pl.loop(0, HEADS)
        def _(k):
            hot[pl.ds(pl.multiple_of(k * n, n), n), t * n : (t + 1) * n] = jnp.where(
                slots + k * n == row, 1.0, 0.0
            ).astype(BF)

        for j in range(HEADS * n // 128):
            hot_t[t * n : (t + 1) * n, j * 128 : (j + 1) * 128] = jnp.where(
                lanes + j * 128 == column, 1.0, 0.0
            ).astype(BF)

    arrived(got_u, U, half)
    for t in range(HEADS):
        packed = got_u[t * half : (t + 1) * half, :]
        tile_qku[t * n : t * n + half, PAIR : PAIR + HEAD] = packed[:, :HEAD]
        tile_qku[t * n + half : (t + 1) * n, PAIR : PAIR + HEAD] = packed[:, HEAD:]
    tile_qku[:, PAIR + HEAD :] = jnp.zeros((HEADS * n, HEAD), BF)
    arrived(got_qk, QK, n)
    tile_qku[:, :PAIR] = got_qk[...]

    @pl.loop(0, HEADS)
    def _(k):
        here = pl.ds(pl.multiple_of(k * n, n), n)
        three = jnp.dot(hot[here, :], tile_qku[...], preferred_element_type=F32).astype(BF)
        win_qku[here, :] = three
        queries, keys = three[:, :HEAD], three[:, HEAD:PAIR]
        s = lax.dot_general(keys, queries, NT, preferred_element_type=F32) * scale
        e = jnp.exp(s - jnp.max(s, axis=0, keepdims=True))
        p = e * (1.0 / jnp.sum(e, axis=0, keepdims=True))
        probs[here, :] = p
        d_val[here, :] = jnp.dot(
            p.astype(BF), three[:, PAIR : PAIR + HEAD], preferred_element_type=F32
        ).astype(BF)

    def value_rows(t, target):
        here = pl.ds(pl.multiple_of(t * n, n), n)
        back = jnp.dot(hot_t[here, :], d_val[...], preferred_element_type=F32).astype(BF)
        place = pl.ds(pl.multiple_of(t * half, half), half)
        target[place, :HEAD] = back[:half]
        target[place, HEAD:] = back[half:]

    for t in peers:
        value_rows(t, send_dv)
        remote(block(send_dv, t, half), block(got_dv, me, half), DV + t, DV + me, (dp, t)).start()
    value_rows(me, got_dv)

    arrived(got_v, V, half)
    for t in range(HEADS):
        packed = got_v[t * half : (t + 1) * half, :]
        tile_v[t * n : t * n + half, :] = packed[:, :HEAD]
        tile_v[t * n + half : (t + 1) * n, :] = packed[:, HEAD:]

    @pl.loop(0, HEADS)
    def _(k):
        here = pl.ds(pl.multiple_of(k * n, n), n)
        values = jnp.dot(hot[here, :], tile_v[...], preferred_element_type=F32).astype(BF)
        three = win_qku[here, :]
        p = probs[here, :]
        gp = lax.dot_general(
            values, three[:, PAIR : PAIR + HEAD], NT, preferred_element_type=F32
        )
        delta = jnp.sum(p * gp, axis=0, keepdims=True)
        gs = (p * (gp - delta) * scale).astype(BF)
        queries, keys = three[:, :HEAD], three[:, HEAD:PAIR]
        d_win[here, :HEAD] = lax.dot_general(gs, keys, TN, preferred_element_type=F32).astype(BF)
        d_win[here, HEAD:] = jnp.dot(gs, queries, preferred_element_type=F32).astype(BF)

    def to_tile(t, target):
        here = pl.ds(pl.multiple_of(t * n, n), n)
        target[here, :] = jnp.dot(
            hot_t[here, :], d_win[...], preferred_element_type=F32
        ).astype(BF)

    for t in peers:
        to_tile(t, send_dqk)
        remote(block(send_dqk, t, n), block(got_dqk, me, n), DQK + t, DQK + me, (dp, t)).start()
    to_tile(me, got_dqk)
    depth = acc.shape[1]
    d1, d2, d3, d4 = depth // 2, depth // 4, depth // 8, depth // 32
    b1 = (1 - c) * bx + c * by
    b2 = (1 - c) * by + c * bx
    peer_1 = (1 - c) * peer_x + c * peer_y
    peer_2 = (1 - c) * peer_y + c * peer_x
    off0 = c * d1
    off1 = off0 + b1 * d2
    off2 = off1 + b2 * d3
    off3 = off2 + me * d4
    windows = lax.axis_size("dp") * lax.axis_size("win")

    def at(off, size):
        return pl.ds(pl.multiple_of(off, size), size)

    keep0, keep1, keep2, mine = at(off0, d1), at(off1, d2), at(off2, d3), at(off3, d4)
    other0 = at((1 - c) * d1, d1)
    other1 = at(off0 + (1 - b1) * d2, d2)
    other2 = at(off1 + (1 - b2) * d3, d3)

    def halving0(j):
        return remote(stage.at[j, other0], rb0.at[j], R0 + j, R0 + j, (peer_c, me))

    def halving1(j):
        return remote(stage.at[j, other1], rb1.at[j], R1 + j, R1 + j, (peer_1, me))

    def halving2(j):
        return remote(stage.at[j, other2], rb2.at[j], R2 + j, R2 + j, (peer_2, me))

    def reduce0(j):
        g = lax.dot_general(
            normed[...], rows[:, j * inner : (j + 1) * inner], TN, preferred_element_type=F32
        )
        acc[j] = g
        stage[j] = g.astype(BF)
        halving0(j).start()

    def reduce1(j):
        halving0(j).wait()
        g = acc[j, keep0, :] + rb0[j].astype(F32)
        acc[j, keep0, :] = g
        stage[j, keep0, :] = g.astype(BF)
        halving1(j).start()

    def reduce2(j):
        halving1(j).wait()
        g = acc[j, keep1, :] + rb1[j].astype(F32)
        acc[j, keep1, :] = g
        stage[j, keep1, :] = g.astype(BF)
        halving2(j).start()

    def piece(j, t):
        return stage.at[j, at(off2 + t * d4, d4)]

    def reduce_z(j):
        halving2(j).wait()
        g = acc[j, keep2, :] + rb2[j].astype(F32)
        acc[j, keep2, :] = g
        stage[j, keep2, :] = g.astype(BF)
        for t in peers:
            remote(piece(j, t), rbz.at[j, me], RZ + 4 * j + t, RZ + 4 * j + me, (dp, t)).start()

    def gather_z(j):
        own = acc[j, mine, :]
        for t in peers:
            got = rbz.at[j, t]
            remote(got, got, RZ + 4 * j + t, RZ + 4 * j + t, (dp, t)).wait_recv()
            own += rbz[j, t].astype(F32)
        total[j, mine, :] = (own * (1.0 / windows)).astype(BF)
        done = total.at[j, mine]
        for t in peers:
            remote(done, done, GZ + 4 * j + t, GZ + 4 * j + me, (dp, t)).start()

    def doubling(j, block_, sem, peer):
        return remote(total.at[j, block_], total.at[j, block_], sem + j, sem + j, (peer, me))

    def gather2(j):
        for t in peers:
            there = total.at[j, at(off2 + t * d4, d4)]
            remote(there, there, GZ + 4 * j + t, GZ + 4 * j + t, (dp, t)).wait_recv()
        doubling(j, keep2, G2, peer_2).start()

    def gather1(j):
        doubling(j, keep2, G2, peer_2).wait_send()
        doubling(j, other2, G2, peer_2).wait_recv()
        doubling(j, keep1, G1, peer_1).start()

    def gather0(j):
        doubling(j, keep1, G1, peer_1).wait_send()
        doubling(j, other1, G1, peer_1).wait_recv()
        doubling(j, keep0, G0, peer_c).start()

    def finish_gather(j):
        doubling(j, keep0, G0, peer_c).wait_send()
        doubling(j, other0, G0, peer_c).wait_recv()
        gw_out[:, j * inner : (j + 1) * inner] = total[j]

    arrived(got_dv, DV, half)
    for h in range(HEADS):
        v_at = 2 * inner + h * HEAD
        rows[:half, v_at : v_at + HEAD] = got_dv[h * half : (h + 1) * half, :HEAD]
        rows[half:, v_at : v_at + HEAD] = got_dv[h * half : (h + 1) * half, HEAD:]
    reduce0(2)
    reduce1(2)
    reduce2(2)
    reduce_z(2)

    arrived(got_dqk, DQK, n)
    for h in range(HEADS):
        rows[:, h * HEAD : (h + 1) * HEAD] = got_dqk[h * n : (h + 1) * n, :HEAD]
        rows[:, inner + h * HEAD : inner + (h + 1) * HEAD] = got_dqk[h * n : (h + 1) * n, HEAD:]
    reduce0(0)
    reduce0(1)
    reduce1(0)
    reduce1(1)

    gn = lax.dot_general(rows[...], w[...], NT, preferred_element_type=F32)
    u = unit[...]
    row_id = lax.broadcasted_iota(jnp.int32, (8, gn.shape[1]), 0)
    small_send[0] = jnp.where(
        row_id == 0,
        jnp.sum(gn * u, axis=0, keepdims=True),
        jnp.where(row_id == 1, jnp.sum(gn, axis=0, keepdims=True), 0.0),
    )
    small0 = remote(small_send.at[0], small_got.at[0], S0, S0, (peer_c, me))
    small0.start()
    reduce2(0)
    reduce2(1)
    gather_z(2)
    gh = gn * gain[...]
    first = jnp.mean(gh, axis=1, keepdims=True)
    second = jnp.mean(gh * u, axis=1, keepdims=True)
    grad_in[...] = (inv[...] * (gh - first - u * second)).astype(BF)

    small0.wait()
    small_send[1] = small_send[0] + small_got[0]
    small1 = remote(small_send.at[1], small_got.at[1], S1, S1, (peer_x, me))
    small1.start()
    reduce_z(0)
    reduce_z(1)
    gather2(2)
    small1.wait()
    small_send[2] = small_send[1] + small_got[1]
    small2 = remote(small_send.at[2], small_got.at[2], S2, S2, (peer_y, me))
    small2.start()
    gather_z(0)
    gather_z(1)
    gather1(2)
    small2.wait()
    small_send[3] = small_send[2] + small_got[2]
    for t in peers:
        remote(small_send.at[3], small_z.at[me], SZ + t, SZ + me, (dp, t)).start()
    small_z[me] = small_send[3]
    gather2(0)
    gather2(1)
    gather0(2)
    gather1(0)
    gather1(1)
    finish_gather(2)
    gather0(0)
    gather0(1)
    for t in peers:
        remote(small_z.at[t], small_z.at[t], SZ + t, SZ + t, (dp, t)).wait_recv()
    gs_out[...] = (small_z[0] + small_z[1] + small_z[2] + small_z[3]) * (1.0 / windows)
    finish_gather(0)
    finish_gather(1)

    for t in peers:
        remote(pos, pos, POS + t, POS + t, (dp, t)).wait_send()
        remote(block(send_qk, t, n), block(send_qk, t, n), QK + t, QK + t, (dp, t)).wait_send()
        remote(block(send_u, t, half), block(send_u, t, half), U + t, U + t, (dp, t)).wait_send()
        remote(block(send_v, t, half), block(send_v, t, half), V + t, V + t, (dp, t)).wait_send()
        remote(block(send_dqk, t, n), block(send_dqk, t, n), DQK + t, DQK + t, (dp, t)).wait_send()
        remote(block(send_dv, t, half), block(send_dv, t, half), DV + t, DV + t, (dp, t)).wait_send()
        for j in range(3):
            done = total.at[j, mine]
            remote(piece(j, t), piece(j, t), RZ + 4 * j + t, RZ + 4 * j + t, (dp, t)).wait_send()
            remote(done, done, GZ + 4 * j + t, GZ + 4 * j + t, (dp, t)).wait_send()
        remote(small_send.at[3], small_send.at[3], SZ + t, SZ + t, (dp, t)).wait_send()


def by_heads(features, upstream_grad, window_of, window_slot, gain, bias, w_qkv):
    n, width = features.shape[1:]
    cols = w_qkv.shape[1]
    all_rows = HEADS * n
    pos = jnp.broadcast_to(window_of * n + window_slot, (8, n))
    vmem = pl.BlockSpec(memory_space=pltpu.VMEM)
    grad_in, grad_w, small = pl.pallas_call(
        fused,
        out_shape=(
            jax.ShapeDtypeStruct((n, width), BF),
            jax.ShapeDtypeStruct((width, cols), BF),
            jax.ShapeDtypeStruct((8, width), F32),
        ),
        in_specs=[vmem] * 6,
        out_specs=(vmem, vmem, vmem),
        scratch_shapes=[
            pltpu.VMEM((n, width), F32),
            pltpu.VMEM((n, width), BF),
            pltpu.VMEM((n, 1), F32),
            pltpu.VMEM((HEADS, 8, n), jnp.int32),
            pltpu.VMEM((all_rows, PAIR), BF),
            pltpu.VMEM((all_rows // 2, PAIR), BF),
            pltpu.VMEM((all_rows // 2, PAIR), BF),
            pltpu.VMEM((all_rows, PAIR), BF),
            pltpu.VMEM((all_rows // 2, PAIR), BF),
            pltpu.VMEM((all_rows // 2, PAIR), BF),
            pltpu.VMEM((all_rows, 2 * PAIR), BF),
            pltpu.VMEM((all_rows, HEAD), BF),
            pltpu.VMEM((all_rows, all_rows), BF),
            pltpu.VMEM((all_rows, all_rows), BF),
            pltpu.VMEM((all_rows, 2 * PAIR), BF),
            pltpu.VMEM((all_rows, n), F32),
            pltpu.VMEM((all_rows, HEAD), BF),
            pltpu.VMEM((all_rows, PAIR), BF),
            pltpu.VMEM((all_rows, PAIR), BF),
            pltpu.VMEM((all_rows // 2, PAIR), BF),
            pltpu.VMEM((all_rows, PAIR), BF),
            pltpu.VMEM((all_rows // 2, PAIR), BF),
            pltpu.VMEM((n, cols), BF),
            pltpu.VMEM((3, width, cols // 3), F32),
            pltpu.VMEM((3, width, cols // 3), BF),
            pltpu.VMEM((3, width // 2, cols // 3), BF),
            pltpu.VMEM((3, width // 4, cols // 3), BF),
            pltpu.VMEM((3, width // 8, cols // 3), BF),
            pltpu.VMEM((3, HEADS, width // 32, cols // 3), BF),
            pltpu.VMEM((3, width, cols // 3), BF),
            pltpu.VMEM((4, 8, width), F32),
            pltpu.VMEM((3, 8, width), F32),
            pltpu.VMEM((HEADS, 8, width), F32),
            pltpu.SemaphoreType.DMA((N_SEM,)),
            pltpu.SemaphoreType.DMA((N_SEM,)),
        ],
        compiler_params=pltpu.CompilerParams(
            collective_id=0, has_side_effects=True, vmem_limit_bytes=56 * 2**20
        ),
    )(features[0], upstream_grad[0], pos, gain[None], bias[None], w_qkv)
    return grad_in[None], grad_w.astype(F32), small[0], small[1]


def solution(mesh):
    placed = (
        P("dp", "win", None),
        P("dp", "win", None),
        P("dp", "win"),
        P("dp", "win"),
        P(),
        P(),
        P(),
    )
    heads_fit = mesh.shape["win"] == HEADS and mesh.shape["dp"] == 8
    return jax.shard_map(
        by_heads if heads_fit else per_device,
        mesh=mesh,
        in_specs=placed,
        out_specs=(P("dp", "win", None), P(), P(), P()),
        check_vma=False,
    )
```

```python
import jax
import jax.numpy as jnp
from jax import lax
from jax.experimental import pallas as pl
from jax.experimental.pallas import tpu as pltpu
from jax.sharding import PartitionSpec as P

HEADS = 4
HEAD = 64


epsilon = 1e-05


def normalize(window_rows, gain, bias, w_qkv):
    rows_f = window_rows.astype(jnp.float32)
    row_mean = jnp.mean(rows_f, axis=1, keepdims=True)
    centered = rows_f - row_mean
    row_var = jnp.mean(centered * centered, axis=1, keepdims=True)
    inv_std = lax.rsqrt(row_var + epsilon)
    unit_rows = centered * inv_std
    normed = (unit_rows * gain + bias).astype(jnp.bfloat16)
    qkv = jnp.dot(normed, w_qkv, preferred_element_type=jnp.float32).astype(jnp.bfloat16)
    return (unit_rows, inv_std, normed, qkv)


def attention_grads(qkv, window_upstream):
    inner = HEADS * HEAD
    score_scale = HEAD ** (-0.5)
    d_queries = []
    d_keys = []
    d_values = []
    for head_num in range(HEADS):
        col_start = head_num * HEAD
        queries = qkv[:, col_start : col_start + HEAD]
        key_block = qkv[:, inner + col_start : inner + col_start + HEAD]
        value_block = qkv[:, 2 * inner + col_start : 2 * inner + col_start + HEAD]
        outer = window_upstream[:, col_start : col_start + HEAD]
        scores = jnp.dot(queries, key_block.T, preferred_element_type=jnp.float32) * score_scale
        row_max = jnp.max(scores, axis=1, keepdims=True)
        exp_scores = jnp.exp(scores - row_max)
        attn_probs = exp_scores / jnp.sum(exp_scores, axis=1, keepdims=True)
        probs_bf = attn_probs.astype(jnp.bfloat16)
        grad_probs = jnp.dot(outer, value_block.T, preferred_element_type=jnp.float32)
        row_delta = jnp.sum(attn_probs * grad_probs, axis=1, keepdims=True)
        grad_scores = (attn_probs * (grad_probs - row_delta) * score_scale).astype(jnp.bfloat16)
        d_queries.append(
            jnp.dot(grad_scores, key_block, preferred_element_type=jnp.float32).astype(jnp.bfloat16)
        )
        d_keys.append(
            lax.dot_general(
                grad_scores, queries, (((0,), (0,)), ((), ())), preferred_element_type=jnp.float32
            ).astype(jnp.bfloat16)
        )
        d_values.append(
            lax.dot_general(
                probs_bf, outer, (((0,), (0,)), ((), ())), preferred_element_type=jnp.float32
            ).astype(jnp.bfloat16)
        )
    return jnp.concatenate(d_queries + d_keys + d_values, axis=1)


def finish(grad_rows, unit_rows, inv_std, normed, gain, w_qkv):
    grad_weight = lax.dot_general(
        normed, grad_rows, (((0,), (0,)), ((), ())), preferred_element_type=jnp.float32
    )
    grad_normed = lax.dot_general(
        grad_rows, w_qkv, (((1,), (1,)), ((), ())), preferred_element_type=jnp.float32
    )
    grad_gain = jnp.sum(grad_normed * unit_rows, axis=0)
    grad_bias = jnp.sum(grad_normed, axis=0)
    grad_hat = grad_normed * gain
    first_mean = jnp.mean(grad_hat, axis=1, keepdims=True)
    second_mean = jnp.mean(grad_hat * unit_rows, axis=1, keepdims=True)
    grad_window = (inv_std * (grad_hat - first_mean - unit_rows * second_mean)).astype(jnp.bfloat16)
    return (grad_window, grad_weight, grad_gain, grad_bias)


def per_device(features, upstream_grad, window_of, window_slot, gain, bias, w_qkv):
    win_count = lax.axis_size("win")
    point_count = features.shape[1]
    model_width = features.shape[2]
    inner = upstream_grad.shape[2]
    capacity = 2 * point_count // win_count
    tile_rows = features[0]
    tile_upstream = upstream_grad[0]
    target = window_of[0]
    slot_in = window_slot[0]
    point = jnp.arange(point_count, dtype=jnp.int32)
    earlier = (target[None, :] == target[:, None]) & (point[None, :] < point[:, None])
    send_rank = jnp.sum(earlier.astype(jnp.int32), axis=1)
    position = target * capacity + send_rank
    send_rows = (
        jnp.zeros((win_count * capacity, model_width), jnp.bfloat16).at[position].set(tile_rows)
    )
    send_rows = send_rows.reshape(win_count, capacity, model_width)
    send_slots = jnp.full((win_count * capacity,), point_count, jnp.int32).at[position].set(slot_in)
    send_slots = send_slots.reshape(win_count, capacity)
    send_upstream = (
        jnp.zeros((win_count * capacity, inner), jnp.bfloat16).at[position].set(tile_upstream)
    )
    send_upstream = send_upstream.reshape(win_count, capacity, inner)
    got_rows, got_slots, got_upstream = (
        lax.all_to_all(send_rows, "win", split_axis=0, concat_axis=0, tiled=True),
        lax.all_to_all(send_slots, "win", split_axis=0, concat_axis=0, tiled=True),
        lax.all_to_all(send_upstream, "win", split_axis=0, concat_axis=0, tiled=True),
    )
    flat_slots = got_slots.reshape(-1)
    arrival = (
        jnp.zeros((point_count,), jnp.int32)
        .at[flat_slots]
        .set(jnp.arange(win_count * capacity, dtype=jnp.int32), mode="drop")
    )
    window_rows = got_rows.reshape(-1, model_width)[arrival]
    unit_rows, inv_std, normed, qkv = normalize(window_rows, gain, bias, w_qkv)
    window_upstream = got_upstream.reshape(-1, inner)[arrival]
    grad_rows = attention_grads(qkv, window_upstream)
    grad_window, grad_weight, grad_gain, grad_bias = finish(
        grad_rows, unit_rows, inv_std, normed, gain, w_qkv
    )
    live = (flat_slots < point_count)[:, None]
    safe_slots = jnp.minimum(flat_slots, point_count - 1)
    send_back = jnp.where(live, grad_window[safe_slots], jnp.zeros((), jnp.bfloat16))
    send_back = send_back.reshape(win_count, capacity, model_width)
    returned = lax.all_to_all(send_back, "win", split_axis=0, concat_axis=0, tiled=True)
    grad_in = returned.reshape(-1, model_width)[position]
    total_weight, total_gain, total_bias = lax.psum(
        (grad_weight, grad_gain, grad_bias), ("dp", "win")
    )
    window_count = lax.axis_size("dp") * win_count
    return (
        grad_in[None],
        total_weight / window_count,
        total_gain / window_count,
        total_bias / window_count,
    )


BF = jnp.bfloat16
F32 = jnp.float32
PAIR = 2 * HEAD
NT = (((1,), (1,)), ((), ()))
TN = (((0,), (0,)), ((), ()))

POS, QK, U, V, DQK, DV, SZ = (4 * i for i in range(7))
S0, S1, S2 = 28, 29, 30
R0, R1, R2, G0, G1, G2 = (31 + 3 * i for i in range(6))
RZ, GZ = 49, 61
N_SEM = 73


def fused(
    feat,
    up,
    window,
    slot,
    gain,
    bias,
    w,
    grad_in,
    gw_out,
    gs_out,
    unit,
    normed,
    inv,
    pos_all,
    send_qk,
    send_u,
    send_v,
    got_qk,
    got_u,
    got_v,
    tile_qku,
    tile_v,
    hot,
    hot_t,
    win_qku,
    probs,
    d_val,
    d_win,
    send_dqk,
    send_dv,
    got_dqk,
    got_dv,
    rows,
    acc,
    stage,
    rb0,
    rb1,
    rb2,
    rbz,
    total,
    small_send,
    small_got,
    small_z,
    ssem,
    rsem,
):
    n = feat.shape[0]
    half = n // 2
    inner = HEADS * HEAD
    scale = HEAD ** (-0.5)
    dp = lax.axis_index("dp")
    me = lax.axis_index("win")
    c = dp % 2
    bx = (dp // 2) % 2
    by = dp // 4
    peer_c = dp + 1 - 2 * c
    peer_x = dp + 2 - 4 * bx
    peer_y = dp + 4 - 8 * by
    peers = [(me + d) % HEADS for d in (2, 1, 3)]

    def remote(source, target, s, r, where):
        return pltpu.make_async_remote_copy(
            src_ref=source,
            dst_ref=target,
            send_sem=ssem.at[s],
            recv_sem=rsem.at[r],
            device_id=where,
            device_id_type=pl.DeviceIdType.MESH,
        )

    places = [(dp, t) for t in peers] + [(p, me) for p in (peer_c, peer_x, peer_y)]
    barrier = pltpu.get_barrier_semaphore()
    for place in places:
        pl.semaphore_signal(barrier, inc=1, device_id=place, device_id_type=pl.DeviceIdType.MESH)
    pl.semaphore_wait(barrier, len(places))

    def block(ref, t, size):
        return ref.at[pl.ds(pl.multiple_of(t * size, size), size)]

    def exchange(source, target, base, size):
        for t in peers:
            remote(block(source, t, size), block(target, me, size), base + t, base + me, (dp, t)).start()

    def arrived(target, base, size):
        for t in peers:
            remote(block(target, t, size), block(target, t, size), base + t, base + t, (dp, t)).wait_recv()

    pos_all[me] = jnp.broadcast_to(window[...] * n + slot[...], (8, n))
    for t in peers:
        remote(pos_all.at[me], pos_all.at[me], POS + t, POS + me, (dp, t)).start()

    for h in range(HEADS):
        send_u[h * half : (h + 1) * half, :HEAD] = up[:half, h * HEAD : (h + 1) * HEAD]
        send_u[h * half : (h + 1) * half, HEAD:] = up[half:, h * HEAD : (h + 1) * HEAD]
    exchange(send_u, got_u, U, half)

    x = feat[...].astype(F32)
    centered = x - jnp.mean(x, axis=1, keepdims=True)
    inv_std = lax.rsqrt(jnp.mean(centered * centered, axis=1, keepdims=True) + epsilon)
    u = centered * inv_std
    unit[...] = u
    inv[...] = inv_std
    normed[...] = (u * gain[...] + bias[...]).astype(BF)
    qk = jnp.dot(normed[...], w[:, : 2 * inner], preferred_element_type=F32).astype(BF)
    for h in range(HEADS):
        send_qk[h * n : (h + 1) * n, :HEAD] = qk[:, h * HEAD : (h + 1) * HEAD]
        send_qk[h * n : (h + 1) * n, HEAD:] = qk[:, inner + h * HEAD : inner + (h + 1) * HEAD]
    exchange(send_qk, got_qk, QK, n)
    v = jnp.dot(normed[...], w[:, 2 * inner :], preferred_element_type=F32).astype(BF)
    for h in range(HEADS):
        send_v[h * half : (h + 1) * half, :HEAD] = v[:half, h * HEAD : (h + 1) * HEAD]
        send_v[h * half : (h + 1) * half, HEAD:] = v[half:, h * HEAD : (h + 1) * HEAD]
    exchange(send_v, got_v, V, half)
    mine = pl.ds(pl.multiple_of(me * n, n), n)
    got_qk[mine, :] = send_qk[mine, :]
    mine = pl.ds(pl.multiple_of(me * half, half), half)
    got_u[mine, :] = send_u[mine, :]
    got_v[mine, :] = send_v[mine, :]

    for t in peers:
        remote(pos_all.at[t], pos_all.at[t], POS + t, POS + t, (dp, t)).wait_recv()
    for t in range(HEADS):
        row = jnp.broadcast_to(pos_all[t, 0:1, :], (128, n))
        column = row.astype(F32).T.astype(jnp.int32)
        row = jnp.broadcast_to(pos_all[t, 0:1, :], (n, n))
        slots = lax.broadcasted_iota(jnp.int32, (n, n), 0)
        lanes = lax.broadcasted_iota(jnp.int32, (n, 128), 1)

        @pl.loop(0, HEADS)
        def _(k):
            hot[pl.ds(pl.multiple_of(k * n, n), n), t * n : (t + 1) * n] = jnp.where(
                slots + k * n == row, 1.0, 0.0
            ).astype(BF)

        for j in range(HEADS * n // 128):
            hot_t[t * n : (t + 1) * n, j * 128 : (j + 1) * 128] = jnp.where(
                lanes + j * 128 == column, 1.0, 0.0
            ).astype(BF)

    arrived(got_u, U, half)
    for t in range(HEADS):
        packed = got_u[t * half : (t + 1) * half, :]
        tile_qku[t * n : t * n + half, PAIR : PAIR + HEAD] = packed[:, :HEAD]
        tile_qku[t * n + half : (t + 1) * n, PAIR : PAIR + HEAD] = packed[:, HEAD:]
    tile_qku[:, PAIR + HEAD :] = jnp.zeros((HEADS * n, HEAD), BF)
    arrived(got_qk, QK, n)
    tile_qku[:, :PAIR] = got_qk[...]

    @pl.loop(0, HEADS)
    def _(k):
        here = pl.ds(pl.multiple_of(k * n, n), n)
        three = jnp.dot(hot[here, :], tile_qku[...], preferred_element_type=F32).astype(BF)
        win_qku[here, :] = three
        queries, keys = three[:, :HEAD], three[:, HEAD:PAIR]
        s = lax.dot_general(keys, queries, NT, preferred_element_type=F32) * scale
        e = jnp.exp(s - jnp.max(s, axis=0, keepdims=True))
        p = e * (1.0 / jnp.sum(e, axis=0, keepdims=True))
        probs[here, :] = p
        d_val[here, :] = jnp.dot(
            p.astype(BF), three[:, PAIR : PAIR + HEAD], preferred_element_type=F32
        ).astype(BF)

    def value_rows(t, target):
        here = pl.ds(pl.multiple_of(t * n, n), n)
        back = jnp.dot(hot_t[here, :], d_val[...], preferred_element_type=F32).astype(BF)
        place = pl.ds(pl.multiple_of(t * half, half), half)
        target[place, :HEAD] = back[:half]
        target[place, HEAD:] = back[half:]

    for t in peers:
        value_rows(t, send_dv)
        remote(block(send_dv, t, half), block(got_dv, me, half), DV + t, DV + me, (dp, t)).start()
    value_rows(me, got_dv)

    arrived(got_v, V, half)
    for t in range(HEADS):
        packed = got_v[t * half : (t + 1) * half, :]
        tile_v[t * n : t * n + half, :] = packed[:, :HEAD]
        tile_v[t * n + half : (t + 1) * n, :] = packed[:, HEAD:]

    @pl.loop(0, HEADS)
    def _(k):
        here = pl.ds(pl.multiple_of(k * n, n), n)
        values = jnp.dot(hot[here, :], tile_v[...], preferred_element_type=F32).astype(BF)
        three = win_qku[here, :]
        p = probs[here, :]
        gp = lax.dot_general(
            values, three[:, PAIR : PAIR + HEAD], NT, preferred_element_type=F32
        )
        delta = jnp.sum(p * gp, axis=0, keepdims=True)
        gs = (p * (gp - delta) * scale).astype(BF)
        queries, keys = three[:, :HEAD], three[:, HEAD:PAIR]
        d_win[here, :HEAD] = lax.dot_general(gs, keys, TN, preferred_element_type=F32).astype(BF)
        d_win[here, HEAD:] = jnp.dot(gs, queries, preferred_element_type=F32).astype(BF)

    def to_tile(t, target):
        here = pl.ds(pl.multiple_of(t * n, n), n)
        target[here, :] = jnp.dot(
            hot_t[here, :], d_win[...], preferred_element_type=F32
        ).astype(BF)

    for t in peers:
        to_tile(t, send_dqk)
        remote(block(send_dqk, t, n), block(got_dqk, me, n), DQK + t, DQK + me, (dp, t)).start()
    to_tile(me, got_dqk)
    depth = acc.shape[1]
    d1, d2, d3, d4 = depth // 2, depth // 4, depth // 8, depth // 32
    b1 = (1 - c) * bx + c * by
    b2 = (1 - c) * by + c * bx
    peer_1 = (1 - c) * peer_x + c * peer_y
    peer_2 = (1 - c) * peer_y + c * peer_x
    off0 = c * d1
    off1 = off0 + b1 * d2
    off2 = off1 + b2 * d3
    off3 = off2 + me * d4
    windows = lax.axis_size("dp") * lax.axis_size("win")

    def at(off, size):
        return pl.ds(pl.multiple_of(off, size), size)

    keep0, keep1, keep2, mine = at(off0, d1), at(off1, d2), at(off2, d3), at(off3, d4)
    other0 = at((1 - c) * d1, d1)
    other1 = at(off0 + (1 - b1) * d2, d2)
    other2 = at(off1 + (1 - b2) * d3, d3)

    def halving0(j):
        return remote(stage.at[j, other0], rb0.at[j], R0 + j, R0 + j, (peer_c, me))

    def halving1(j):
        return remote(stage.at[j, other1], rb1.at[j], R1 + j, R1 + j, (peer_1, me))

    def halving2(j):
        return remote(stage.at[j, other2], rb2.at[j], R2 + j, R2 + j, (peer_2, me))

    def reduce0(j):
        g = lax.dot_general(
            normed[...], rows[:, j * inner : (j + 1) * inner], TN, preferred_element_type=F32
        )
        acc[j] = g
        stage[j] = g.astype(BF)
        halving0(j).start()

    def reduce1(j):
        halving0(j).wait()
        g = acc[j, keep0, :] + rb0[j].astype(F32)
        acc[j, keep0, :] = g
        stage[j, keep0, :] = g.astype(BF)
        halving1(j).start()

    def reduce2(j):
        halving1(j).wait()
        g = acc[j, keep1, :] + rb1[j].astype(F32)
        acc[j, keep1, :] = g
        stage[j, keep1, :] = g.astype(BF)
        halving2(j).start()

    def piece(j, t):
        return stage.at[j, at(off2 + t * d4, d4)]

    def reduce_z(j):
        halving2(j).wait()
        g = acc[j, keep2, :] + rb2[j].astype(F32)
        acc[j, keep2, :] = g
        stage[j, keep2, :] = g.astype(BF)
        for t in peers:
            remote(piece(j, t), rbz.at[j, me], RZ + 4 * j + t, RZ + 4 * j + me, (dp, t)).start()

    def gather_z(j):
        own = acc[j, mine, :]
        for t in peers:
            got = rbz.at[j, t]
            remote(got, got, RZ + 4 * j + t, RZ + 4 * j + t, (dp, t)).wait_recv()
            own += rbz[j, t].astype(F32)
        total[j, mine, :] = (own * (1.0 / windows)).astype(BF)
        done = total.at[j, mine]
        for t in peers:
            remote(done, done, GZ + 4 * j + t, GZ + 4 * j + me, (dp, t)).start()

    def doubling(j, block_, sem, peer):
        return remote(total.at[j, block_], total.at[j, block_], sem + j, sem + j, (peer, me))

    def gather2(j):
        for t in peers:
            there = total.at[j, at(off2 + t * d4, d4)]
            remote(there, there, GZ + 4 * j + t, GZ + 4 * j + t, (dp, t)).wait_recv()
        doubling(j, keep2, G2, peer_2).start()

    def gather1(j):
        doubling(j, keep2, G2, peer_2).wait_send()
        doubling(j, other2, G2, peer_2).wait_recv()
        doubling(j, keep1, G1, peer_1).start()

    def gather0(j):
        doubling(j, keep1, G1, peer_1).wait_send()
        doubling(j, other1, G1, peer_1).wait_recv()
        doubling(j, keep0, G0, peer_c).start()

    def finish_gather(j):
        doubling(j, keep0, G0, peer_c).wait_send()
        doubling(j, other0, G0, peer_c).wait_recv()
        gw_out[:, j * inner : (j + 1) * inner] = total[j]

    arrived(got_dv, DV, half)
    for h in range(HEADS):
        v_at = 2 * inner + h * HEAD
        rows[:half, v_at : v_at + HEAD] = got_dv[h * half : (h + 1) * half, :HEAD]
        rows[half:, v_at : v_at + HEAD] = got_dv[h * half : (h + 1) * half, HEAD:]
    reduce0(2)
    reduce1(2)
    reduce2(2)
    reduce_z(2)

    arrived(got_dqk, DQK, n)
    for h in range(HEADS):
        rows[:, h * HEAD : (h + 1) * HEAD] = got_dqk[h * n : (h + 1) * n, :HEAD]
        rows[:, inner + h * HEAD : inner + (h + 1) * HEAD] = got_dqk[h * n : (h + 1) * n, HEAD:]
    reduce0(0)
    reduce0(1)
    reduce1(0)
    reduce1(1)

    gn = lax.dot_general(rows[...], w[...], NT, preferred_element_type=F32)
    u = unit[...]
    row_id = lax.broadcasted_iota(jnp.int32, (8, gn.shape[1]), 0)
    small_send[0] = jnp.where(
        row_id == 0,
        jnp.sum(gn * u, axis=0, keepdims=True),
        jnp.where(row_id == 1, jnp.sum(gn, axis=0, keepdims=True), 0.0),
    )
    small0 = remote(small_send.at[0], small_got.at[0], S0, S0, (peer_c, me))
    small0.start()
    reduce2(0)
    reduce2(1)
    gather_z(2)
    gh = gn * gain[...]
    first = jnp.mean(gh, axis=1, keepdims=True)
    second = jnp.mean(gh * u, axis=1, keepdims=True)
    grad_in[...] = (inv[...] * (gh - first - u * second)).astype(BF)

    small0.wait()
    small_send[1] = small_send[0] + small_got[0]
    small1 = remote(small_send.at[1], small_got.at[1], S1, S1, (peer_x, me))
    small1.start()
    reduce_z(0)
    reduce_z(1)
    gather2(2)
    small1.wait()
    small_send[2] = small_send[1] + small_got[1]
    small2 = remote(small_send.at[2], small_got.at[2], S2, S2, (peer_y, me))
    small2.start()
    gather_z(0)
    gather_z(1)
    gather1(2)
    small2.wait()
    small_send[3] = small_send[2] + small_got[2]
    for t in peers:
        remote(small_send.at[3], small_z.at[me], SZ + t, SZ + me, (dp, t)).start()
    small_z[me] = small_send[3]
    gather2(0)
    gather2(1)
    gather0(2)
    gather1(0)
    gather1(1)
    finish_gather(2)
    gather0(0)
    gather0(1)
    for t in peers:
        remote(small_z.at[t], small_z.at[t], SZ + t, SZ + t, (dp, t)).wait_recv()
    gs_out[...] = (small_z[0] + small_z[1] + small_z[2] + small_z[3]) * (1.0 / windows)
    finish_gather(0)
    finish_gather(1)

    for t in peers:
        remote(pos_all.at[me], pos_all.at[me], POS + t, POS + t, (dp, t)).wait_send()
        remote(block(send_qk, t, n), block(send_qk, t, n), QK + t, QK + t, (dp, t)).wait_send()
        remote(block(send_u, t, half), block(send_u, t, half), U + t, U + t, (dp, t)).wait_send()
        remote(block(send_v, t, half), block(send_v, t, half), V + t, V + t, (dp, t)).wait_send()
        remote(block(send_dqk, t, n), block(send_dqk, t, n), DQK + t, DQK + t, (dp, t)).wait_send()
        remote(block(send_dv, t, half), block(send_dv, t, half), DV + t, DV + t, (dp, t)).wait_send()
        for j in range(3):
            done = total.at[j, mine]
            remote(piece(j, t), piece(j, t), RZ + 4 * j + t, RZ + 4 * j + t, (dp, t)).wait_send()
            remote(done, done, GZ + 4 * j + t, GZ + 4 * j + t, (dp, t)).wait_send()
        remote(small_send.at[3], small_send.at[3], SZ + t, SZ + t, (dp, t)).wait_send()


def by_heads(features, upstream_grad, window_of, window_slot, gain, bias, w_qkv):
    n, width = features.shape[1:]
    cols = w_qkv.shape[1]
    all_rows = HEADS * n
    vmem = pl.BlockSpec(memory_space=pltpu.VMEM)
    grad_in, grad_w, small = pl.pallas_call(
        fused,
        out_shape=(
            jax.ShapeDtypeStruct((n, width), BF),
            jax.ShapeDtypeStruct((width, cols), BF),
            jax.ShapeDtypeStruct((8, width), F32),
        ),
        in_specs=[vmem] * 7,
        out_specs=(vmem, vmem, vmem),
        scratch_shapes=[
            pltpu.VMEM((n, width), F32),
            pltpu.VMEM((n, width), BF),
            pltpu.VMEM((n, 1), F32),
            pltpu.VMEM((HEADS, 8, n), jnp.int32),
            pltpu.VMEM((all_rows, PAIR), BF),
            pltpu.VMEM((all_rows // 2, PAIR), BF),
            pltpu.VMEM((all_rows // 2, PAIR), BF),
            pltpu.VMEM((all_rows, PAIR), BF),
            pltpu.VMEM((all_rows // 2, PAIR), BF),
            pltpu.VMEM((all_rows // 2, PAIR), BF),
            pltpu.VMEM((all_rows, 2 * PAIR), BF),
            pltpu.VMEM((all_rows, HEAD), BF),
            pltpu.VMEM((all_rows, all_rows), BF),
            pltpu.VMEM((all_rows, all_rows), BF),
            pltpu.VMEM((all_rows, 2 * PAIR), BF),
            pltpu.VMEM((all_rows, n), F32),
            pltpu.VMEM((all_rows, HEAD), BF),
            pltpu.VMEM((all_rows, PAIR), BF),
            pltpu.VMEM((all_rows, PAIR), BF),
            pltpu.VMEM((all_rows // 2, PAIR), BF),
            pltpu.VMEM((all_rows, PAIR), BF),
            pltpu.VMEM((all_rows // 2, PAIR), BF),
            pltpu.VMEM((n, cols), BF),
            pltpu.VMEM((3, width, cols // 3), F32),
            pltpu.VMEM((3, width, cols // 3), BF),
            pltpu.VMEM((3, width // 2, cols // 3), BF),
            pltpu.VMEM((3, width // 4, cols // 3), BF),
            pltpu.VMEM((3, width // 8, cols // 3), BF),
            pltpu.VMEM((3, HEADS, width // 32, cols // 3), BF),
            pltpu.VMEM((3, width, cols // 3), BF),
            pltpu.VMEM((4, 8, width), F32),
            pltpu.VMEM((3, 8, width), F32),
            pltpu.VMEM((HEADS, 8, width), F32),
            pltpu.SemaphoreType.DMA((N_SEM,)),
            pltpu.SemaphoreType.DMA((N_SEM,)),
        ],
        compiler_params=pltpu.CompilerParams(
            collective_id=0, has_side_effects=True, vmem_limit_bytes=56 * 2**20
        ),
    )(features[0], upstream_grad[0], window_of, window_slot, gain[None], bias[None], w_qkv)
    return grad_in[None], grad_w.astype(F32), small[0], small[1]


def solution(mesh):
    placed = (
        P("dp", "win", None),
        P("dp", "win", None),
        P("dp", "win"),
        P("dp", "win"),
        P(),
        P(),
        P(),
    )
    heads_fit = mesh.shape["win"] == HEADS and mesh.shape["dp"] == 8
    return jax.shard_map(
        by_heads if heads_fit else per_device,
        mesh=mesh,
        in_specs=placed,
        out_specs=(P("dp", "win", None), P(), P(), P()),
        check_vma=False,
    )
```
